32 devices in a mesh: fsdp: 2 (over x), ctx: 4 (over z), tp: 4 (over y, core).
Axes of the slice: x: 2, y: 2, z: 4, core: 2. Of those that a mesh axis runs over, the one named last changes fastest.
Arguments:
- hidden_in: bfloat16 [16384, 1792], P(('fsdp', 'ctx', 'tp')), may hold values from -6 to 6
- cotangent: bfloat16 [16384, 1792], P(('fsdp', 'ctx', 'tp')), may hold values from -6 to 6
- lengths: int32 [2, 4], replicated, may hold values from 1024 to 2048, as said below
- to_model: int32 [16384], P(('fsdp', 'ctx', 'tp')), may hold values from 0 to 16383, as said below
- to_loader: int32 [16384], P(('fsdp', 'ctx', 'tp')), may hold values from 0 to 16383, as said below
- conv_in: bfloat16 [1792, 2, 1792], P(('fsdp', 'ctx'), None, 'tp'), may hold values from -0.125 to 0.125
- conv_kernel: float32 [3, 1792], replicated, may hold values from -4.5 to 4.5
- conv_out: bfloat16 [1792, 1792], P('tp', ('fsdp', 'ctx')), may hold values from -0.375 to 0.375
- ffn_one_in: bfloat16 [1792, 2, 4864], P(('fsdp', 'ctx'), None, 'tp'), may hold values from -0.125 to 0.125
- ffn_one_out: bfloat16 [4864, 1792], P('tp', ('fsdp', 'ctx')), may hold values from -0.078125 to 0.078125
- attn_in: bfloat16 [1792, 16, 144], P(('fsdp', 'ctx'), 'tp'), may hold values from -0.125 to 0.125
- attn_out: bfloat16 [1792, 1792], P('tp', ('fsdp', 'ctx')), may hold values from -1 to 1
- ffn_two_in: bfloat16 [1792, 2, 4864], P(('fsdp', 'ctx'), None, 'tp'), may hold values from -0.125 to 0.125
- ffn_two_out: bfloat16 [4864, 1792], P('tp', ('fsdp', 'ctx')), may hold values from -0.078125 to 0.078125
- gains: float32 [4, 1792], replicated, may hold values from 0.5 to 1.5
Outputs:
- hidden_out: bfloat16 [16384, 1792], P(('fsdp', 'ctx', 'tp'))
- grad_in: bfloat16 [16384, 1792], P(('fsdp', 'ctx', 'tp'))
- grad_conv_in: float32 [1792, 2, 1792], P(('fsdp', 'ctx'), None, 'tp')
- grad_conv_kernel: float32 [3, 1792], replicated
- grad_conv_out: float32 [1792, 1792], P('tp', ('fsdp', 'ctx'))
- grad_ffn_one_in: float32 [1792, 2, 4864], P(('fsdp', 'ctx'), None, 'tp')
- grad_ffn_one_out: float32 [4864, 1792], P('tp', ('fsdp', 'ctx'))
- grad_attn_in: float32 [1792, 16, 144], P(('fsdp', 'ctx'), 'tp')
- grad_attn_out: float32 [1792, 1792], P('tp', ('fsdp', 'ctx'))
- grad_ffn_two_in: float32 [1792, 2, 4864], P(('fsdp', 'ctx'), None, 'tp')
- grad_ffn_two_out: float32 [4864, 1792], P('tp', ('fsdp', 'ctx'))
- grad_gains: float32 [4, 1792], replicated
The draws below stay inside these ranges and needn't reach their ends.
Inputs may be any that keep to these rules, and one draw needn't show every extreme that they name: `lengths`: in each of the 2 rows one sequence, at a place drawn from the seed, has length exactly 2048. `to_model`: A permutation of the 16384 rows that keeps every row within its index of fsdp; every device receives exactly 32 rows from each device of its index of fsdp. `to_loader`: the inverse permutation of to_model.
All inputs are finite; a program needn't handle non-finite values.
Results may differ from the reference program's by a relative error of at most 0.015.
Values may be sent and summed in bfloat16 or wider, within the bound.
No kernel may reach another device: no remote copies, remote signals or barrier semaphores. Data moves between devices by JAX's collectives and lax.ppermute only.
A program may use at most 280 MiB of HBM per device.

```python
import jax
import jax.numpy as jnp
from jax import lax

D = 1792
H = 16
F = 16
FF = 4864
DH = 112
MAXLEN = 2048
MINLEN = 1024
SEQS = 4
SLOT = 512
ROWS_DEV = 512
TOKENS = 16384
N_FSDP = 2
N_CTX = 4
N_TP = 4


def route_tables(key):
    key = jax.random.fold_in(key, 7)
    group_size = N_CTX * N_TP
    per_peer = ROWS_DEV // group_size
    first_key, second_key = jax.random.split(key)
    slot_keys = jax.random.split(first_key, N_FSDP * group_size)
    slots = jax.vmap(lambda each: jax.random.permutation(each, ROWS_DEV))(slot_keys)
    slots = slots.reshape(N_FSDP, group_size, group_size, per_peer)
    order_keys = jax.random.split(second_key, N_FSDP * group_size)
    orders = jax.vmap(lambda each: jax.random.permutation(each, ROWS_DEV))(order_keys)
    orders = orders.reshape(N_FSDP, group_size, ROWS_DEV)
    source = orders // per_peer
    within = orders % per_peer
    fsdp_idx = jnp.arange(N_FSDP, dtype=jnp.int32)[:, None, None]
    dest_idx = jnp.arange(group_size, dtype=jnp.int32)[None, :, None]
    local = slots[fsdp_idx, source, dest_idx, within]
    forward = ((fsdp_idx * group_size + source) * ROWS_DEV + local).reshape(-1).astype(jnp.int32)
    backward = jnp.argsort(forward).astype(jnp.int32)
    return (forward, backward)


def draw_lengths(key, part):
    key = jax.random.fold_in(key, 11)
    first_key, second_key = jax.random.split(key)
    spans = jax.random.randint(first_key, (N_FSDP, SEQS), MINLEN, MAXLEN + 1)
    longest = jax.random.randint(second_key, (N_FSDP, 1), 0, SEQS)
    picked = jnp.arange(SEQS)[None, :] == longest
    return jnp.where(picked, MAXLEN, spans).astype(jnp.int32)


def draw_to_model(key, part):
    forward, backward = route_tables(key)
    return forward


def draw_to_loader(key, part):
    forward, backward = route_tables(key)
    return backward


def with_spikes(values, key, source, target, parts, factor):
    owner, partner = [(jnp.arange(values.shape[axis_at]) // (values.shape[axis_at] // parts)).reshape([-1 if axis == axis_at else 1 for axis in range(values.ndim)]) for axis_at in (source, target)]
    chosen = jax.random.permutation(key, parts)[partner]
    strong = (owner == chosen) | (owner == (partner + parts // 2) % parts)
    return jnp.where(strong, factor * values, values)


def shard_levels(own_key, shape, shards, smallest, largest):
    factor_of = 1.0
    for axis_at, parts in shards:
        steps = jax.random.uniform(jax.random.fold_in(jax.random.fold_in(own_key, 6), axis_at), (parts,), jnp.float32, smallest / len(shards), largest / len(shards))
        factor_of = factor_of * jnp.repeat(jnp.exp(steps), shape[axis_at] // parts).reshape((-1,) + (1,) * (len(shape) - 1 - axis_at))
    return factor_of


def normal_values(stream_key, extent, spread, most, cuts=(), kind=jnp.bfloat16):
    loudness = shard_levels(stream_key, extent, cuts, -0.22, 0.18) if cuts else 1.0
    entries = jax.random.normal(stream_key, extent, jnp.float32) * spread * loudness
    return jnp.minimum(jnp.maximum(entries, -most), most).astype(kind)


def noise_with(stream_key, extent, scale, most, pieces, heavy, kind=jnp.bfloat16):
    drawn = scale * jax.random.normal(stream_key, extent, jnp.float32)
    if pieces:
        drawn = drawn * shard_levels(stream_key, extent, pieces, -0.22, 0.18)
    return jnp.clip(with_spikes(drawn, jax.random.fold_in(stream_key, 3), *heavy), -most, most).astype(kind)


def setup_inputs(seed: int = 0) -> dict:
    splits = jax.random.split(jax.random.key(seed), 16)
    hidden_in = noise_with(splits[0], (TOKENS, D), 1.0, 6.0, ((0, 32),), (0, 1, 32, 2.75))
    cotangent = normal_values(splits[1], (TOKENS, D), 1.0, 6.0, ((0, 32),))
    lengths = draw_lengths(jax.random.fold_in(splits[15], 71), 0)
    to_model = draw_to_model(jax.random.fold_in(splits[15], 71), 0)
    to_loader = draw_to_loader(jax.random.fold_in(splits[15], 71), 0)
    conv_in = normal_values(splits[5], (D, 2, D), D ** -0.5, 0.125, ((0, 8), (2, 4)))
    conv_kernel = normal_values(splits[6], (3, D), 1.5, 4.5, (), jnp.float32)
    conv_out = normal_values(splits[7], (D, D), (D // 8) ** -0.5, 0.375, ((0, 4), (1, 8)))
    ffn_one_in = normal_values(splits[8], (D, 2, FF), D ** -0.5, 0.125, ((0, 8), (2, 4)))
    ffn_one_out = normal_values(splits[9], (FF, D), FF ** -0.5, 0.078125, ((0, 4), (1, 8)))
    attn_in = normal_values(splits[10], (D, H, 2 * F + DH), D ** -0.5, 0.125, ((0, 8), (1, 4)))
    attn_out = normal_values(splits[11], (D, D), (D // 64) ** -0.5, 1.0, ((0, 4), (1, 8)))
    ffn_two_in = normal_values(splits[12], (D, 2, FF), D ** -0.5, 0.125, ((0, 8), (2, 4)))
    ffn_two_out = normal_values(splits[13], (FF, D), FF ** -0.5, 0.078125, ((0, 4), (1, 8)))
    gains = jnp.clip(1.0 + 0.1 * jax.random.normal(splits[14], (4, D), jnp.float32), 0.5, 1.5)
    return dict(hidden_in=hidden_in, cotangent=cotangent, lengths=lengths, to_model=to_model, to_loader=to_loader, conv_in=conv_in, conv_kernel=conv_kernel, conv_out=conv_out, ffn_one_in=ffn_one_in, ffn_one_out=ffn_one_out, attn_in=attn_in, attn_out=attn_out, ffn_two_in=ffn_two_in, ffn_two_out=ffn_two_out, gains=gains)


@jax.custom_vjp
def low(v):
    return lax.optimization_barrier(v.astype(jnp.bfloat16)).astype(jnp.float32)

@jax.custom_vjp
def low_back(v):
    return v

def low_keep(v):
    return (low(v), None)

def low_pass(kept, grad):
    return (grad,)

def back_keep(v):
    return (v, None)

def back_low(kept, grad):
    return (low(grad),)
low.defvjp(low_keep, low_pass)
low_back.defvjp(back_keep, back_low)
highest_precision = lax.Precision.HIGHEST
epsilon = 1e-05
quad_scale = 0.7071067811865476

def features(vector):
    quad = (vector[..., :, None] * vector[..., None, :]).reshape(vector.shape[:-1] + (vector.shape[-1] * vector.shape[-1],)) * quad_scale
    return jnp.concatenate([quad, vector, jnp.ones(vector.shape[:-1] + (1,), jnp.float32)], axis=-1)

def rms_norm(stream, gain):
    scaled = stream * lax.rsqrt(lax.optimization_barrier(jnp.mean(stream * stream, axis=-1, keepdims=True)) + epsilon)
    return low(scaled * gain)

def conv_branch(rms_normalized_input, input_weight, kernel, output_weight):
    projected_features = low_back(jnp.einsum('vey,yij->veij', rms_normalized_input, input_weight, precision=highest_precision))
    signal = low(projected_features[:, :, 0])
    gate_value = projected_features[:, :, 1]
    one_back = jnp.pad(signal, ((0, 0), (1, 0), (0, 0)))[:, :-1]
    two_back = jnp.pad(signal, ((0, 0), (2, 0), (0, 0)))[:, :-2]
    mixture = kernel[0] * signal + kernel[1] * one_back + kernel[2] * two_back
    hidden_activation = low(mixture * gate_value)
    return low_back(jnp.einsum('mqo,oz->mqz', hidden_activation, output_weight, precision=highest_precision))

def ffn_branch(rms_normalized_input, input_weight, output_weight):
    projected_features = low_back(jnp.einsum('cta,azq->ctzq', rms_normalized_input, input_weight, precision=highest_precision))
    hidden_activation = low(jax.nn.silu(projected_features[:, :, 0]) * projected_features[:, :, 1])
    return low_back(jnp.einsum('uwn,nv->uwv', hidden_activation, output_weight, precision=highest_precision))

def attend(queries, key_rows, values):
    span = MAXLEN // N_CTX

    def blocked(tensor):
        return tensor.reshape(N_CTX, span, tensor.shape[1], tensor.shape[2])
    q_block, k_block, v_block = (blocked(queries), blocked(key_rows), blocked(values))
    extended = jnp.concatenate([v_block, jnp.ones(v_block.shape[:-1] + (1,), jnp.float32)], axis=-1)
    scores = low_back(jnp.einsum('bphf,bqhf->bhpq', q_block, k_block, precision=highest_precision))
    causal = jnp.arange(span)[:, None] >= jnp.arange(span)[None, :]
    weight = low(jnp.where(causal, 1.0 + scores + 0.5 * scores * scores, 0.0))
    q_feat = low(features(q_block))
    k_feat = low(features(k_block))
    states = low_back(jnp.einsum('bqhe,bqhv->bhev', k_feat, extended, precision=highest_precision))
    earlier = low(jnp.concatenate([jnp.zeros_like(states[:1]), jnp.cumsum(states[:-1], axis=0)], axis=0))
    totals = low_back(jnp.einsum('bhpq,bqhv->bphv', weight, extended, precision=highest_precision) + jnp.einsum('bphe,bhev->bphv', q_feat, earlier, precision=highest_precision))
    result = low(totals[..., :-1] / totals[..., -1:])
    return result.reshape(MAXLEN, -1)

def attn_branch(rms_normalized_input, input_weight, output_weight):
    projected_features = low_back(jnp.einsum('uma,ayk->umyk', rms_normalized_input, input_weight, precision=highest_precision))
    queries = low(0.5 * projected_features[..., :F])
    key_rows = low(0.5 * projected_features[..., F:2 * F])
    values = low(projected_features[..., 2 * F:])
    single = jax.checkpoint(lambda packed: attend(*packed))
    per_head_output = lax.map(single, (queries, key_rows, values))
    return low_back(jnp.einsum('mqo,oz->mqz', per_head_output, output_weight, precision=highest_precision))

def to_sequences(rows_arr):
    width = rows_arr.shape[-1]
    shaped = rows_arr.reshape(N_FSDP, N_CTX, SEQS, SLOT, width).transpose(0, 2, 1, 3, 4)
    return shaped.reshape(N_FSDP * SEQS, MAXLEN, width)

def to_rows(seq_arr):
    width = seq_arr.shape[-1]
    shaped = seq_arr.reshape(N_FSDP, SEQS, N_CTX, SLOT, width).transpose(0, 2, 1, 3, 4)
    return shaped.reshape(TOKENS, width)

def reference(hidden_in, cotangent, lengths, to_model, to_loader, conv_in, conv_kernel, conv_out, ffn_one_in, ffn_one_out, attn_in, attn_out, ffn_two_in, ffn_two_out, gains):
    positions = jnp.arange(MAXLEN, dtype=jnp.int32)
    valid = (positions[None, :] < lengths.reshape(-1)[:, None]).astype(jnp.float32)[:, :, None]
    stream_in = to_sequences(hidden_in.astype(jnp.float32)[to_model])
    cotan_seq = to_sequences(cotangent.astype(jnp.float32)[to_model])
    params = tuple((weight.astype(jnp.float32) for weight in (conv_in, conv_kernel, conv_out, ffn_one_in, ffn_one_out, attn_in, attn_out, ffn_two_in, ffn_two_out, gains)))

    def forward(stream, c_in, kernel, c_out, f1_in, f1_out, a_in, a_out, f2_in, f2_out, gain_rows):
        stream = stream + valid * conv_branch(rms_norm(stream, gain_rows[0]), c_in, kernel, c_out)
        stream = stream + valid * ffn_branch(rms_norm(stream, gain_rows[1]), f1_in, f1_out)
        stream = stream + valid * attn_branch(rms_norm(stream, gain_rows[2]), a_in, a_out)
        stream = stream + valid * ffn_branch(rms_norm(stream, gain_rows[3]), f2_in, f2_out)
        return stream
    result, pull = jax.vjp(forward, stream_in, *params)
    grads = pull(cotan_seq)
    hidden_out = to_rows(result)[to_loader].astype(jnp.bfloat16)
    grad_in = to_rows(grads[0])[to_loader].astype(jnp.bfloat16)
    return (hidden_out, grad_in, grads[1], grads[2], grads[3], grads[4], grads[5], grads[6], grads[7], grads[8], grads[9], grads[10])
```

```python
import jax
import jax.numpy as jnp
import numpy as np
from jax import lax
from jax.experimental import pallas as pl
from jax.experimental.pallas import tpu as pltpu
from jax.sharding import Mesh, PartitionSpec as P

F = 16
MAXLEN = 2048

epsilon = 1e-05
quad_scale = 0.7071067811865476
WEIGHT_AXES = ("y", "fsdp", "ctx")
LAYER_AXES = ("fsdp", "ctx")
bf16 = jnp.bfloat16
f32 = jnp.float32


def from_behind(block, axis, distance):
    devices = range(lax.axis_size(axis))
    route = [(i - distance, i) for i in devices if i - distance in devices]
    return lax.ppermute(block, axis, route)


def running_sum(part, direction):
    window = part
    total = jnp.zeros(part.shape, f32)
    step = 1
    while step < lax.axis_size("ctx"):
        arrived = from_behind(window.astype(bf16), "ctx", direction * step).astype(f32)
        total = total + arrived
        window = window + arrived
        step *= 2
    return (total * TIMES[:, None]).astype(bf16)


def sum_everywhere(value):
    for axis in ("core", "y", "fsdp", "ctx"):
        step = 1
        size = lax.axis_size(axis)
        while step < size:
            value = value + lax.ppermute(value, axis, [(i, i ^ step) for i in range(size)])
            step *= 2
    return value


PAIRS = [(a, b) for a in range(F) for b in range(a, F)]
FIRST = np.array([[float(a == i) for a, b in PAIRS] for i in range(F)], np.float32)
SECOND = np.array([[float(b == i) for a, b in PAIRS] for i in range(F)], np.float32)
TIMES = np.array([2.0 if a < b else 1.0 for a, b in PAIRS] + [1.0] * (F + 1), np.float32)


def features(vector):
    quad = jnp.dot(vector, FIRST) * jnp.dot(vector, SECOND) * quad_scale
    return jnp.concatenate([quad, vector, jnp.ones(vector.shape[:-1] + (1,), f32)], axis=-1)


def norm_rows(stream, gain):
    return stream * lax.rsqrt(jnp.mean(stream * stream, axis=-1, keepdims=True) + epsilon) * gain


def slot_index(peer, order_key, per_peer):
    same = peer[:, None] == peer[None, :]
    before = order_key[None, :] < order_key[:, None]
    return peer * per_peer + jnp.sum((same & before).astype(jnp.int32), axis=1)


def regroup(rows, order, position):
    received = lax.all_to_all(
        rows[order], ("ctx", "y", "core"), split_axis=0, concat_axis=0, tiled=True
    )
    return received[position]


def core_swap(value):
    return lax.ppermute(value, "core", [(0, 1), (1, 0)])


def gather_weight(weight):
    whole = lax.all_gather(weight, WEIGHT_AXES, axis=0, tiled=True)
    return whole.reshape(lax.axis_size("y"), -1, weight.shape[1])


def gather_slice(weight):
    return lax.all_gather(weight, LAYER_AXES, axis=0, tiled=True)


def scatter_grad(grad, axes):
    flat = grad.astype(bf16).reshape(-1, grad.shape[-1])
    return lax.psum_scatter(flat, axes, scatter_dimension=0, tiled=True).astype(f32)


def tie(*values):
    return lax.optimization_barrier(values)


def after(value, *others):
    for other in others:
        corner = other.reshape((-1,) + other.shape[-2:])[0, :16, :128]
        first = lax.optimization_barrier(corner)[:1, :1].reshape(())
        value = value + (first * 0).astype(value.dtype)
    return value


def bit_of(axis, step):
    return lax.axis_index(axis) // step % 2


def swap(value, axis, step):
    return lax.ppermute(value, axis, [(i, i ^ step) for i in range(lax.axis_size(axis))])


def pick(value, index, dim):
    return lax.dynamic_index_in_dim(value, index, dim, keepdims=False)


def halve_start(value, axis):
    size = lax.axis_size(axis)
    dims = size.bit_length() - 1
    value = value.reshape((2,) * dims + value.shape[1:])
    bit = bit_of(axis, 1)
    return pick(value, bit, dims - 1), swap(pick(value, 1 - bit, dims - 1), axis, 1)


def halve_rest(kept, arrived, axis):
    size = lax.axis_size(axis) // 2
    value = (kept.astype(f32) + arrived.astype(f32)).astype(bf16)
    dims = size.bit_length() - 1
    return halve(value.reshape((size,) + value.shape[dims:]), axis, 2)


def halve(value, axis, done=1):
    size = lax.axis_size(axis) // done
    dims = size.bit_length() - 1
    value = value.reshape((2,) * dims + value.shape[1:])
    for dim in reversed(range(dims)):
        bit = bit_of(axis, done)
        other = swap(pick(value, 1 - bit, dim), axis, done)
        value = (pick(value, bit, dim).astype(f32) + other.astype(f32)).astype(bf16)
        done *= 2
    return value


def half_columns(rows, bit, fsdp):
    width = rows.shape[1] // fsdp
    if fsdp == 2:
        return lax.dynamic_slice_in_dim(rows, bit * width, width, 1)
    parts = rows.reshape(-1, fsdp // 2, 2, width)
    return pick(parts, bit, 2).reshape(-1, fsdp // 2 * width)


def reduce_start(rows, value):
    fsdp = lax.axis_size("fsdp")
    theirs = slice_grad(half_columns(rows, 1 - bit_of("fsdp", 1), fsdp), value)
    return swap(theirs.astype(bf16), "fsdp", 1)


def reduce_middle(rows, value, arrived):
    fsdp, ctx = (lax.axis_size(axis) for axis in LAYER_AXES)
    k = value.shape[-1]
    mine = slice_grad(half_columns(rows, bit_of("fsdp", 1), fsdp), value)
    total = (mine + arrived.astype(f32)).astype(bf16)
    total = halve(total.reshape(fsdp // 2, ctx, -1, k), "fsdp", 2)
    return halve_start(total, "ctx")


def reduce_grad(rows, value, first):
    fsdp, ctx, y = (lax.axis_size(axis) for axis in ("fsdp", "ctx", "y"))
    k = value.shape[-1]
    d = rows.shape[1] // (fsdp * ctx)
    bit = bit_of(first, 1)
    if first == "y":
        parts = value.reshape(y // 2, 2, -1, k)
        theirs = weight_grad(rows, pick(parts, 1 - bit, 1)).astype(bf16)
        mine = weight_grad(rows, pick(parts, bit, 1))
    else:
        theirs = weight_grad(half_columns(rows, 1 - bit, fsdp), value)
        mine = weight_grad(half_columns(rows, bit, fsdp), value)
        theirs = theirs.astype(bf16)
    total = (mine + swap(theirs, first, 1).astype(f32)).astype(bf16)
    if first == "y":
        total = halve(total.reshape(y // 2, fsdp, ctx, d, k), "y", 2)
        total = halve(total, "fsdp")
    else:
        total = total.reshape(y, fsdp // 2, ctx, d, k).swapaxes(0, 1)
        total = halve(halve(total, "fsdp", 2), "y")
    return halve(total, "ctx").astype(f32)


class Rows:
    def __init__(self, row_count, slot_rows):
        self.count = row_count
        self.own_first = row_count % slot_rows == 0
        self.core = lax.axis_index("core")

    def spread(self, own):
        other = core_swap(own)
        if self.own_first:
            return jnp.concatenate([own, other], axis=0)
        low = jnp.where(self.core == 0, own, other)
        high = jnp.where(self.core == 0, other, own)
        return jnp.concatenate([low, high], axis=0)

    def halves(self, value):
        if self.own_first:
            return value[:, : self.count], value[:, self.count :]
        own = lax.dynamic_slice_in_dim(value, self.core * self.count, self.count, 1)
        other = lax.dynamic_slice_in_dim(value, (1 - self.core) * self.count, self.count, 1)
        return own, other

    def collect(self, value, weight):
        own, other = self.halves(value)
        theirs = jnp.einsum("yrk,ydk->rd", other, weight, preferred_element_type=f32).astype(bf16)
        arrived = core_swap(theirs)
        mine = jnp.einsum("yrk,ydk->rd", own, weight, preferred_element_type=f32)
        return mine + arrived.astype(f32)


def spread_wide(own, *meanwhile):
    value = own[None]
    step = 1
    while step < lax.axis_size("y"):
        arrived, *meanwhile = tie(swap(value, "y", step), *meanwhile)
        value = jnp.concatenate([value, arrived], axis=0)
        step *= 2
    other = core_swap(value)
    value = jnp.concatenate([value, other], axis=0).reshape(-1, own.shape[-1])
    return (value, *meanwhile) if meanwhile else value


def products_wide(value, weight):
    y = lax.axis_size("y")
    blocks = value.reshape(2, y, -1, value.shape[-1])
    count = blocks.shape[2]

    def part(block):
        flat = block.reshape(-1, block.shape[-1])
        return jnp.einsum("rk,dk->rd", flat, weight, preferred_element_type=f32)

    far = part(blocks[:, 1:]).reshape(2, y - 1, count, -1)
    far = far[0] + core_swap(far[1].astype(bf16)).astype(f32)
    extra = 0.0
    step = y // 2
    while step > 1:
        arrived = swap(far[step - 1 :].astype(bf16), "y", step).astype(f32)
        extra = extra + arrived[0]
        far = far[: step - 1] + arrived[1:]
        step //= 2
    near = part(blocks[:, 0]).reshape(2, count, -1)
    return far[0].astype(bf16), near[0] + extra, near[1].astype(bf16)


def collect_wide(value, weight, *meanwhile):
    far, near, neighbour = products_wide(value, weight)
    arrived, near, neighbour, *meanwhile = tie(swap(far, "y", 1), near, neighbour, *meanwhile)
    total = near + core_swap(neighbour).astype(f32) + arrived.astype(f32)
    return (total, *meanwhile) if meanwhile else total


def slice_project(rows, weight):
    return jnp.einsum("rd,dk->rk", rows, weight, preferred_element_type=f32)


def slice_grad(rows, value):
    return jnp.einsum("rd,rk->dk", rows, value, preferred_element_type=f32)


def project(normed, weight):
    return jnp.einsum("rd,ydk->yrk", normed, weight, preferred_element_type=f32)


def weight_grad(rows, value):
    return jnp.einsum("rd,yrk->ydk", rows, value, preferred_element_type=f32)


def split_sequences(value, slot_rows):
    return value.reshape(value.shape[0], -1, slot_rows, value.shape[-1])


def join_sequences(value):
    return value.reshape(value.shape[0], -1, value.shape[-1])


def conv_forward(normed, w_in, kernel, slot_rows):
    z = split_sequences(project(normed, w_in), slot_rows)
    ch = z.shape[-1] // 2
    signal = z[..., :ch].astype(bf16)
    gate = z[..., ch:]
    before = from_behind(signal[:, :, slot_rows - 2 :], "ctx", 1)
    widened = jnp.concatenate([before, signal], axis=2).astype(f32)
    taps = (widened[:, :, 2:], widened[:, :, 1:-1], widened[:, :, :-2])
    k = kernel[:, :, None, None, :]
    mixture = k[0] * taps[0] + k[1] * taps[1] + k[2] * taps[2]
    hidden = join_sequences((mixture * gate).astype(bf16))
    return hidden, (widened.astype(bf16), gate)


def conv_backward(grad_out, w_out, kernel, stored, slot_rows):
    widened, gate = stored
    widened = widened.astype(f32)
    taps = (widened[:, :, 2:], widened[:, :, 1:-1], widened[:, :, :-2])
    k = kernel[:, :, None, None, :]
    mixture = k[0] * taps[0] + k[1] * taps[1] + k[2] * taps[2]
    grad_hidden = split_sequences(project(grad_out, w_out), slot_rows)
    grad_mix = grad_hidden * gate
    grad_gate = grad_hidden * mixture
    after = from_behind(grad_mix[:, :, :2], "ctx", -1)
    wide = jnp.concatenate([grad_mix, after], axis=2)
    grad_signal = k[0] * grad_mix + k[1] * wide[:, :, 1:-1] + k[2] * wide[:, :, 2:]
    grad_kernel = jnp.stack([jnp.sum(grad_mix * tap, axis=(1, 2)) for tap in taps])
    grad_signal = join_sequences(grad_signal.astype(bf16))
    grad_gate = join_sequences(grad_gate.astype(bf16))
    return grad_signal, grad_gate, grad_kernel


def ffn_forward(normed, w_in):
    z = lax.optimization_barrier(slice_project(normed, w_in).astype(bf16))
    f = z.shape[-1] // 2
    hidden = (jax.nn.silu(z[..., :f].astype(f32)) * z[..., f:].astype(f32)).astype(bf16)
    return hidden, z


def swiglu_grad_kernel(grad_ref, weight_ref, z_ref, out_ref):
    f = weight_ref.shape[1]
    grad_hidden = jnp.dot(grad_ref[...], weight_ref[...], preferred_element_type=f32)
    z = z_ref[...].astype(f32)
    gate, up = z[:, :f], z[:, f:]
    s = 1.0 / (1.0 + jnp.exp(-gate))
    out_ref[:, :f] = (grad_hidden * up * (s * (1.0 + gate * (1.0 - s)))).astype(bf16)
    out_ref[:, f:] = (grad_hidden * (gate * s)).astype(bf16)


def ffn_backward(grad_out, w_out, z):
    count, width = grad_out.shape
    f = w_out.shape[1]
    block = 256
    return pl.pallas_call(
        swiglu_grad_kernel,
        grid=(count // block,),
        in_specs=[
            pl.BlockSpec((block, width), lambda i: (i, 0)),
            pl.BlockSpec((width, f), lambda i: (0, 0)),
            pl.BlockSpec((block, 2 * f), lambda i: (i, 0)),
        ],
        out_specs=pl.BlockSpec((block, 2 * f), lambda i: (i, 0)),
        out_shape=jax.ShapeDtypeStruct((count, 2 * f), bf16),
        cost_estimate=pl.CostEstimate(
            flops=2 * count * width * f,
            bytes_accessed=2 * (count * width + width * f + 4 * count * f),
            transcendentals=count * f,
        ),
        compiler_params=pltpu.CompilerParams(vmem_limit_bytes=56 * 2**20),
    )(grad_out, w_out, z)


def pair_grad_kernel(rows_ref, first_ref, grad_ref, second_ref, out_ref):
    split = first_ref.shape[1]
    down = (((0,), (0,)), ((), ()))
    out_ref[:, :split] = lax.dot_general(
        rows_ref[...], first_ref[...], down, preferred_element_type=f32
    ).astype(bf16)
    out_ref[:, split:] = lax.dot_general(
        grad_ref[...], second_ref[...], down, preferred_element_type=f32
    ).astype(bf16)


def pair_grad(rows, first, grad, second):
    count, width = rows.shape
    a, b = first.shape[1], second.shape[1]
    block = 256
    return pl.pallas_call(
        pair_grad_kernel,
        grid=(width // block,),
        in_specs=[
            pl.BlockSpec((count, block), lambda i: (0, i)),
            pl.BlockSpec((count, a), lambda i: (0, 0)),
            pl.BlockSpec((count, block), lambda i: (0, i)),
            pl.BlockSpec((count, b), lambda i: (0, 0)),
        ],
        out_specs=pl.BlockSpec((block, a + b), lambda i: (i, 0)),
        out_shape=jax.ShapeDtypeStruct((width, a + b), bf16),
        cost_estimate=pl.CostEstimate(
            flops=2 * count * width * (a + b),
            bytes_accessed=2 * (2 * count * width + (count + width) * (a + b)),
            transcendentals=0,
        ),
        compiler_params=pltpu.CompilerParams(vmem_limit_bytes=56 * 2**20),
    )(rows, first, grad, second)


def causal_mask(slot_rows):
    return jnp.arange(slot_rows)[:, None] >= jnp.arange(slot_rows)[None, :]


def to_heads(z, heads):
    y, s, l, width = z.shape
    return z.reshape(y, s, l, heads, width // heads).transpose(0, 1, 3, 2, 4)


def from_heads(value):
    y, s, h, l, e = value.shape
    return value.transpose(0, 1, 3, 2, 4).reshape(y, s * l, h * e)


def attn_forward(normed, w_in, heads, slot_rows):
    z = split_sequences(project(normed, w_in), slot_rows)
    queries = to_heads((0.5 * z[..., : heads * F]).astype(bf16), heads)
    keys = to_heads((0.5 * z[..., heads * F : 2 * heads * F]).astype(bf16), heads)
    values = to_heads(z[..., 2 * heads * F :].astype(bf16), heads)
    extended = jnp.concatenate([values, jnp.ones(values.shape[:-1] + (1,), bf16)], axis=-1)
    k_feat = features(keys.astype(f32)).astype(bf16)
    states = jnp.einsum("...qe,...qv->...ev", k_feat, extended, preferred_element_type=f32)
    earlier = running_sum(states, 1)
    scores = jnp.einsum("...pf,...qf->...pq", queries, keys, preferred_element_type=f32)
    weight = jnp.where(
        causal_mask(slot_rows), 1.0 + scores + 0.5 * scores * scores, 0.0
    ).astype(bf16)
    q_feat = features(queries.astype(f32)).astype(bf16)
    totals = jnp.einsum(
        "...pq,...qv->...pv", weight, extended, preferred_element_type=f32
    ) + jnp.einsum("...pe,...ev->...pv", q_feat, earlier, preferred_element_type=f32)
    out = from_heads((totals[..., :-1] / totals[..., -1:]).astype(bf16))
    return out, (queries, keys, extended, earlier, totals)


def attn_backward(grad_out, w_out, stored, heads, slot_rows):
    (queries, keys, extended, earlier, totals), grad_out = lax.optimization_barrier(
        (stored, grad_out)
    )
    q_feat = features(queries.astype(f32)).astype(bf16)
    k_feat = features(keys.astype(f32)).astype(bf16)
    grad_heads = to_heads(split_sequences(project(grad_out, w_out), slot_rows), heads)
    denominator = totals[..., -1:]
    grad_num = grad_heads / denominator
    grad_den = -jnp.sum(grad_heads * totals[..., :-1], axis=-1, keepdims=True) / (
        denominator * denominator
    )
    grad_total = jnp.concatenate([grad_num, grad_den], axis=-1).astype(bf16)
    grad_prior = jnp.einsum("...pe,...pv->...ev", q_feat, grad_total, preferred_element_type=f32)
    grad_state = running_sum(grad_prior, -1)
    scores = jnp.einsum("...pf,...qf->...pq", queries, keys, preferred_element_type=f32)
    mask = causal_mask(slot_rows)
    weight = jnp.where(mask, 1.0 + scores + 0.5 * scores * scores, 0.0).astype(bf16)
    grad_weight = jnp.einsum("...pv,...qv->...pq", grad_total, extended, preferred_element_type=f32)
    grad_qf = jnp.einsum("...pv,...ev->...pe", grad_total, earlier, preferred_element_type=f32)
    grad_score = jnp.where(mask, grad_weight * (1.0 + scores), 0.0).astype(bf16)
    grad_ext = jnp.einsum(
        "...pq,...pv->...qv", weight, grad_total, preferred_element_type=f32
    ) + jnp.einsum("...qe,...ev->...qv", k_feat, grad_state, preferred_element_type=f32)
    grad_kf = jnp.einsum("...qv,...ev->...qe", extended, grad_state, preferred_element_type=f32)
    unused, pull_query = jax.vjp(features, queries.astype(f32))
    unused, pull_key = jax.vjp(features, keys.astype(f32))
    grad_query = (
        jnp.einsum("...pq,...qf->...pf", grad_score, keys, preferred_element_type=f32)
        + pull_query(grad_qf)[0]
    )
    grad_key = (
        jnp.einsum("...pq,...pf->...qf", grad_score, queries, preferred_element_type=f32)
        + pull_key(grad_kf)[0]
    )
    grad_z = jnp.concatenate(
        [
            from_heads((0.5 * grad_query).astype(bf16)),
            from_heads((0.5 * grad_key).astype(bf16)),
            from_heads(grad_ext[..., :-1].astype(bf16)),
        ],
        axis=-1,
    )
    return grad_z


def norm_back(stream, grad_normed, gain):
    unused, pull = jax.vjp(norm_rows, stream, gain)
    return pull(grad_normed)


def heads_apart(weight):
    d = weight.shape[0]
    return jnp.concatenate(
        [
            weight[..., :F].reshape(d, -1),
            weight[..., F : 2 * F].reshape(d, -1),
            weight[..., 2 * F :].reshape(d, -1),
        ],
        axis=1,
    )


def heads_together(weight, heads):
    d = weight.shape[0]
    q = weight[:, : heads * F].reshape(d, heads, F)
    k = weight[:, heads * F : 2 * heads * F].reshape(d, heads, F)
    v = weight[:, 2 * heads * F :].reshape(d, heads, -1)
    return jnp.concatenate([q, k, v], axis=-1)


def shards(
    hidden_in,
    cotangent,
    lengths,
    to_model,
    to_loader,
    conv_in,
    conv_kernel,
    conv_out,
    ffn_one_in,
    ffn_one_out,
    attn_in,
    attn_out,
    ffn_two_in,
    ffn_two_out,
    gains,
):
    y_size = lax.axis_size("y")
    ctx_size = lax.axis_size("ctx")
    tp_size = 2 * y_size
    group_size = ctx_size * tp_size
    row_count = hidden_in.shape[0]
    per_peer = row_count // group_size
    slot_rows = MAXLEN // ctx_size
    block_rows = row_count * tp_size
    core = lax.axis_index("core")
    tp_rank = lax.axis_index("y") * 2 + core
    heads = attn_in.shape[1]
    rows = Rows(row_count, slot_rows)

    d = conv_in.shape[0]
    conv_width = conv_in.shape[1] * conv_in.shape[2]
    attn_width = heads * attn_in.shape[2]
    attn_start = -(-attn_width // 128) * 128
    c_w = gather_weight(jnp.concatenate([conv_in.reshape(d, -1), conv_out.T], axis=1))
    pad = jnp.zeros((d, attn_start - attn_width), bf16)
    a_w = jnp.concatenate([heads_apart(attn_in), pad, attn_out.T], axis=1)
    ffn_width = ffn_one_in.shape[1] * ffn_one_in.shape[2]
    f1_w = jnp.concatenate([ffn_one_in.reshape(d, -1), ffn_one_out.T], axis=1)
    f2_w = jnp.concatenate([ffn_two_in.reshape(d, -1), ffn_two_out.T], axis=1)

    counter = jnp.arange(row_count, dtype=jnp.int32)
    send_slot = slot_index(to_loader // row_count % group_size, counter, per_peer)
    recv_slot = slot_index(to_model // row_count % group_size, to_model % row_count, per_peer)
    send_order = jnp.argsort(send_slot)
    stream_zero = regroup(hidden_in, send_order, recv_slot)
    f1_w = gather_slice(after(f1_w, c_w, stream_zero))
    a_w = gather_weight(after(a_w, f1_w))
    f2_w = gather_slice(after(f2_w, a_w))
    cotangent = after(cotangent, stream_zero)
    w_c_in, w_c_out = c_w[..., :conv_width], c_w[..., conv_width:]
    w_a_in, w_a_out = a_w[..., :attn_width], a_w[..., attn_start:]
    w_f1_in, w_f1_out = f1_w[:, :ffn_width], f1_w[:, ffn_width:]
    w_f2_in, w_f2_out = f2_w[:, :ffn_width], f2_w[:, ffn_width:]
    cotan_rows = regroup(cotangent, send_order, recv_slot)
    stream_zero = stream_zero.astype(f32)
    seq_lengths = lax.dynamic_index_in_dim(lengths, lax.axis_index("fsdp"), 0, keepdims=False)
    position = lax.axis_index("ctx") * slot_rows + jnp.arange(slot_rows, dtype=jnp.int32)
    valid_block = (position[None, :] < seq_lengths[:, None]).astype(f32).reshape(block_rows)
    valid_rows = lax.dynamic_slice_in_dim(valid_block, tp_rank * row_count, row_count)[:, None]
    channels = conv_in.shape[2]
    kernel = lax.dynamic_index_in_dim(
        conv_kernel.reshape(3, y_size, 2, channels), core, 2, keepdims=False
    )

    def normed_of(stream, index, spread=rows.spread):
        return spread(norm_rows(stream, gains[index]).astype(bf16))

    def grad_rows(carry, spread=rows.spread, *meanwhile):
        return spread((valid_rows * carry).astype(bf16), *meanwhile)

    normed_zero = normed_of(stream_zero, 0)
    hid_zero, stored_zero = conv_forward(normed_zero, w_c_in, kernel, slot_rows)
    stream_one = stream_zero + valid_rows * rows.collect(hid_zero, w_c_out)
    normed_one = normed_of(stream_one, 1, spread_wide)
    upstream = cotan_rows.astype(f32)
    normed_one, grad_out = tie(normed_one, grad_rows(upstream, spread_wide))
    hid_one, z_one = ffn_forward(normed_one, w_f1_in)
    stream_two = stream_one + valid_rows * collect_wide(hid_one, w_f1_out)
    normed_two = normed_of(stream_two, 2)
    hid_two, stored_two = attn_forward(normed_two, w_a_in, heads, slot_rows)
    stream_three = stream_two + valid_rows * rows.collect(hid_two, w_a_out)
    normed_three = normed_of(stream_three, 3, spread_wide)
    hid_three, z_three = ffn_forward(normed_three, w_f2_in)

    grad_z = ffn_backward(grad_out, w_f2_out, z_three)
    g_f2 = pair_grad(normed_three, grad_z, grad_out, hid_three)
    terms, g_f2 = collect_wide(grad_z, w_f2_in, g_f2)
    step, gain_three = norm_back(stream_three, terms, gains[3])
    upstream = upstream + step
    grad_out = grad_rows(upstream)
    grad_z = attn_backward(grad_out, w_a_out, stored_two, heads, slot_rows)
    g_f2 = scatter_grad(g_f2, LAYER_AXES)
    g_f2_in, g_f2_out = g_f2[:, :ffn_width], g_f2[:, ffn_width:]
    g_a_out = reduce_grad(grad_out, hid_two, "fsdp")
    g_a_in = reduce_grad(normed_two, grad_z, "y")
    step, gain_two = norm_back(stream_two, rows.collect(grad_z, w_a_in), gains[2])
    upstream = upstream + step
    upstream, hid_three = tie(upstream, hid_three)
    last_terms = products_wide(hid_three, w_f2_out)
    grad_out, *last_terms = grad_rows(upstream, spread_wide, *last_terms)
    out_arrived = reduce_start(grad_out, hid_one)
    grad_z = ffn_backward(grad_out, w_f1_out, z_one)
    in_arrived = reduce_start(normed_one, grad_z)
    step, gain_one = norm_back(stream_one, collect_wide(grad_z, w_f1_in), gains[1])
    upstream = upstream + step
    own_rows = (valid_rows * upstream).astype(bf16)
    own_rows, out_arrived, *last_terms = tie(own_rows, out_arrived, *last_terms)
    last_arrived = swap(last_terms[0], "y", 1)
    stream_four = last_terms[1] + core_swap(last_terms[2]).astype(f32) + last_arrived.astype(f32)
    stream_four = stream_three + valid_rows * stream_four
    hidden_out = regroup(stream_four.astype(bf16), jnp.argsort(recv_slot), send_slot)
    out_parts = reduce_middle(grad_out, hid_one, out_arrived)
    grad_out = rows.spread(own_rows)
    g_c_out = reduce_grad(grad_out, hid_zero, "fsdp")
    grad_signal, grad_gate, grad_kernel = conv_backward(
        grad_out, w_c_out, kernel, stored_zero, slot_rows
    )
    g_c_gate = reduce_grad(normed_zero, grad_gate, "y")
    grad_signal, in_arrived, g_a_in, g_a_out, *out_parts = tie(
        grad_signal, in_arrived, g_a_in, g_a_out, *out_parts
    )
    g_f1_out = halve_rest(*out_parts, "ctx").astype(f32)
    g_f1_in = halve_rest(*reduce_middle(normed_one, grad_z, in_arrived), "ctx").astype(f32)
    g_c_signal = reduce_grad(normed_zero, grad_signal, "fsdp")
    grad_z = jnp.concatenate([grad_signal, grad_gate], axis=-1)
    step, gain_zero = norm_back(stream_zero, rows.collect(grad_z, w_c_in), gains[0])
    upstream = upstream + step
    grad_in = regroup(upstream.astype(bf16), jnp.argsort(recv_slot), send_slot)

    kernel_full = jnp.where(
        (jnp.arange(2) == core)[None, None, :, None], grad_kernel[:, :, None, :], 0.0
    ).reshape(conv_kernel.shape)
    gain_stack = jnp.stack([gain_zero, gain_one, gain_two, gain_three])
    summed = sum_everywhere(jnp.concatenate([gain_stack, kernel_full], axis=0))
    return (
        hidden_out,
        grad_in,
        jnp.stack([g_c_signal, g_c_gate], axis=1),
        summed[4:],
        g_c_out.T,
        g_f1_in.reshape(ffn_one_in.shape),
        g_f1_out.T,
        heads_together(g_a_in, heads),
        g_a_out.T,
        g_f2_in.reshape(ffn_two_in.shape),
        g_f2_out.T,
        summed[:4],
    )


def solution(mesh):
    fsdp, ctx, tp = mesh.devices.shape
    fine = Mesh(mesh.devices.reshape(fsdp, ctx, tp // 2, 2), ("fsdp", "ctx", "y", "core"))
    everything = ("fsdp", "ctx", "y", "core")
    layer = ("fsdp", "ctx")
    tensor = ("y", "core")
    ins = (
        P(everything, None),
        P(everything, None),
        P(),
        P(everything),
        P(everything),
        P(layer, None, tensor),
        P(),
        P(tensor, layer),
        P(layer, None, tensor),
        P(tensor, layer),
        P(layer, tensor, None),
        P(tensor, layer),
        P(layer, None, tensor),
        P(tensor, layer),
        P(),
    )
    outs = (
        P(everything, None),
        P(everything, None),
        P(layer, None, tensor),
        P(),
        P(tensor, layer),
        P(layer, None, tensor),
        P(tensor, layer),
        P(layer, tensor, None),
        P(tensor, layer),
        P(layer, None, tensor),
        P(tensor, layer),
        P(),
    )
    return jax.shard_map(shards, mesh=fine, in_specs=ins, out_specs=outs, check_vma=False)
```

```python
import jax
import jax.numpy as jnp
import numpy as np
from jax import lax
from jax.experimental import pallas as pl
from jax.experimental.pallas import tpu as pltpu
from jax.sharding import Mesh, PartitionSpec as P

F = 16
MAXLEN = 2048

epsilon = 1e-05
quad_scale = 0.7071067811865476
WEIGHT_AXES = ("y", "fsdp", "ctx")
LAYER_AXES = ("fsdp", "ctx")
bf16 = jnp.bfloat16
f32 = jnp.float32


def from_behind(block, axis, distance):
    devices = range(lax.axis_size(axis))
    route = [(i - distance, i) for i in devices if i - distance in devices]
    return lax.ppermute(block, axis, route)


def running_sum(part, direction):
    window = part
    total = jnp.zeros(part.shape, f32)
    step = 1
    while step < lax.axis_size("ctx"):
        arrived = from_behind(window.astype(bf16), "ctx", direction * step).astype(f32)
        total = total + arrived
        window = window + arrived
        step *= 2
    return (total * TIMES[:, None]).astype(bf16)


def sum_everywhere(value):
    for axis in ("core", "y", "fsdp", "ctx"):
        step = 1
        size = lax.axis_size(axis)
        while step < size:
            value = value + lax.ppermute(value, axis, [(i, i ^ step) for i in range(size)])
            step *= 2
    return value


PAIRS = [(a, b) for a in range(F) for b in range(a, F)]
FIRST = np.array([[float(a == i) for a, b in PAIRS] for i in range(F)], np.float32)
SECOND = np.array([[float(b == i) for a, b in PAIRS] for i in range(F)], np.float32)
TIMES = np.array([2.0 if a < b else 1.0 for a, b in PAIRS] + [1.0] * (F + 1), np.float32)


def features(vector):
    quad = jnp.dot(vector, FIRST) * jnp.dot(vector, SECOND) * quad_scale
    return jnp.concatenate([quad, vector, jnp.ones(vector.shape[:-1] + (1,), f32)], axis=-1)


def norm_rows(stream, gain):
    return stream * lax.rsqrt(jnp.mean(stream * stream, axis=-1, keepdims=True) + epsilon) * gain


def slot_index(peer, order_key, per_peer):
    same = peer[:, None] == peer[None, :]
    before = order_key[None, :] < order_key[:, None]
    return peer * per_peer + jnp.sum((same & before).astype(jnp.int32), axis=1)


def regroup(rows, order, position):
    received = lax.all_to_all(
        rows[order], ("ctx", "y", "core"), split_axis=0, concat_axis=0, tiled=True
    )
    return received[position]


def core_swap(value):
    return lax.ppermute(value, "core", [(0, 1), (1, 0)])


def gather_weight(weight):
    whole = lax.all_gather(weight, WEIGHT_AXES, axis=0, tiled=True)
    return whole.reshape(lax.axis_size("y"), -1, weight.shape[1])


def gather_slice(weight):
    return lax.all_gather(weight, LAYER_AXES, axis=0, tiled=True)


def scatter_grad(grad, axes):
    flat = grad.astype(bf16).reshape(-1, grad.shape[-1])
    return lax.psum_scatter(flat, axes, scatter_dimension=0, tiled=True).astype(f32)


def tie(*values):
    return lax.optimization_barrier(values)


def after(value, *others):
    for other in others:
        corner = other.reshape((-1,) + other.shape[-2:])[0, :16, :128]
        first = lax.optimization_barrier(corner)[:1, :1].reshape(())
        value = value + (first * 0).astype(value.dtype)
    return value


def bit_of(axis, step):
    return lax.axis_index(axis) // step % 2


def swap(value, axis, step):
    return lax.ppermute(value, axis, [(i, i ^ step) for i in range(lax.axis_size(axis))])


def pick(value, index, dim):
    return lax.dynamic_index_in_dim(value, index, dim, keepdims=False)


def halve_start(value, axis):
    size = lax.axis_size(axis)
    dims = size.bit_length() - 1
    value = value.reshape((2,) * dims + value.shape[1:])
    bit = bit_of(axis, 1)
    return pick(value, bit, dims - 1), swap(pick(value, 1 - bit, dims - 1), axis, 1)


def halve_rest(kept, arrived, axis):
    size = lax.axis_size(axis) // 2
    value = (kept.astype(f32) + arrived.astype(f32)).astype(bf16)
    dims = size.bit_length() - 1
    return halve(value.reshape((size,) + value.shape[dims:]), axis, 2)


def halve(value, axis, done=1):
    size = lax.axis_size(axis) // done
    dims = size.bit_length() - 1
    value = value.reshape((2,) * dims + value.shape[1:])
    for dim in reversed(range(dims)):
        bit = bit_of(axis, done)
        other = swap(pick(value, 1 - bit, dim), axis, done)
        value = (pick(value, bit, dim).astype(f32) + other.astype(f32)).astype(bf16)
        done *= 2
    return value


def half_columns(rows, bit, fsdp):
    width = rows.shape[1] // fsdp
    if fsdp == 2:
        return lax.dynamic_slice_in_dim(rows, bit * width, width, 1)
    parts = rows.reshape(-1, fsdp // 2, 2, width)
    return pick(parts, bit, 2).reshape(-1, fsdp // 2 * width)


def reduce_start(rows, value):
    fsdp = lax.axis_size("fsdp")
    theirs = slice_grad(half_columns(rows, 1 - bit_of("fsdp", 1), fsdp), value)
    return swap(theirs.astype(bf16), "fsdp", 1)


def reduce_middle(rows, value, arrived):
    fsdp, ctx = (lax.axis_size(axis) for axis in LAYER_AXES)
    k = value.shape[-1]
    mine = slice_grad(half_columns(rows, bit_of("fsdp", 1), fsdp), value)
    total = (mine + arrived.astype(f32)).astype(bf16)
    total = halve(total.reshape(fsdp // 2, ctx, -1, k), "fsdp", 2)
    return halve_start(total, "ctx")


def reduce_grad(rows, value, first):
    fsdp, ctx, y = (lax.axis_size(axis) for axis in ("fsdp", "ctx", "y"))
    k = value.shape[-1]
    d = rows.shape[1] // (fsdp * ctx)
    bit = bit_of(first, 1)
    if first == "y":
        parts = value.reshape(y // 2, 2, -1, k)
        theirs = weight_grad(rows, pick(parts, 1 - bit, 1)).astype(bf16)
        mine = weight_grad(rows, pick(parts, bit, 1))
    else:
        theirs = weight_grad(half_columns(rows, 1 - bit, fsdp), value)
        mine = weight_grad(half_columns(rows, bit, fsdp), value)
        theirs = theirs.astype(bf16)
    total = (mine + swap(theirs, first, 1).astype(f32)).astype(bf16)
    if first == "y":
        total = halve(total.reshape(y // 2, fsdp, ctx, d, k), "y", 2)
        total = halve(total, "fsdp")
    else:
        total = total.reshape(y, fsdp // 2, ctx, d, k).swapaxes(0, 1)
        total = halve(halve(total, "fsdp", 2), "y")
    return halve(total, "ctx").astype(f32)


class Rows:
    def __init__(self, row_count, slot_rows):
        self.count = row_count
        self.own_first = row_count % slot_rows == 0
        self.core = lax.axis_index("core")

    def spread(self, own):
        other = core_swap(own)
        if self.own_first:
            return jnp.concatenate([own, other], axis=0)
        low = jnp.where(self.core == 0, own, other)
        high = jnp.where(self.core == 0, other, own)
        return jnp.concatenate([low, high], axis=0)

    def halves(self, value):
        if self.own_first:
            return value[:, : self.count], value[:, self.count :]
        own = lax.dynamic_slice_in_dim(value, self.core * self.count, self.count, 1)
        other = lax.dynamic_slice_in_dim(value, (1 - self.core) * self.count, self.count, 1)
        return own, other

    def collect(self, value, weight):
        own, other = self.halves(value)
        theirs = jnp.einsum("yrk,ydk->rd", other, weight, preferred_element_type=f32).astype(bf16)
        arrived = core_swap(theirs)
        mine = jnp.einsum("yrk,ydk->rd", own, weight, preferred_element_type=f32)
        return mine + arrived.astype(f32)


def spread_wide(own, *meanwhile):
    value = own[None]
    step = 1
    while step < lax.axis_size("y"):
        arrived, *meanwhile = tie(swap(value, "y", step), *meanwhile)
        value = jnp.concatenate([value, arrived], axis=0)
        step *= 2
    other = core_swap(value)
    value = jnp.concatenate([value, other], axis=0).reshape(-1, own.shape[-1])
    return (value, *meanwhile) if meanwhile else value


def products_wide(value, weight):
    y = lax.axis_size("y")
    blocks = value.reshape(2, y, -1, value.shape[-1])
    count = blocks.shape[2]

    def part(block):
        flat = block.reshape(-1, block.shape[-1])
        return jnp.einsum("rk,dk->rd", flat, weight, preferred_element_type=f32)

    far = part(blocks[:, 1:]).reshape(2, y - 1, count, -1)
    far = far[0] + core_swap(far[1].astype(bf16)).astype(f32)
    extra = 0.0
    step = y // 2
    while step > 1:
        arrived = swap(far[step - 1 :].astype(bf16), "y", step).astype(f32)
        extra = extra + arrived[0]
        far = far[: step - 1] + arrived[1:]
        step //= 2
    near = part(blocks[:, 0]).reshape(2, count, -1)
    return far[0].astype(bf16), near[0] + extra, near[1].astype(bf16)


def collect_wide(value, weight, *meanwhile):
    far, near, neighbour = products_wide(value, weight)
    arrived, near, neighbour, *meanwhile = tie(swap(far, "y", 1), near, neighbour, *meanwhile)
    total = near + core_swap(neighbour).astype(f32) + arrived.astype(f32)
    return (total, *meanwhile) if meanwhile else total


def slice_project(rows, weight):
    return jnp.einsum("rd,dk->rk", rows, weight, preferred_element_type=f32)


def slice_grad(rows, value):
    return jnp.einsum("rd,rk->dk", rows, value, preferred_element_type=f32)


def project(normed, weight):
    return jnp.einsum("rd,ydk->yrk", normed, weight, preferred_element_type=f32)


def weight_grad(rows, value):
    return jnp.einsum("rd,yrk->ydk", rows, value, preferred_element_type=f32)


def split_sequences(value, slot_rows):
    return value.reshape(value.shape[0], -1, slot_rows, value.shape[-1])


def join_sequences(value):
    return value.reshape(value.shape[0], -1, value.shape[-1])


def conv_forward(normed, w_in, kernel, slot_rows):
    z = split_sequences(project(normed, w_in), slot_rows)
    ch = z.shape[-1] // 2
    signal = z[..., :ch].astype(bf16)
    gate = z[..., ch:]
    before = from_behind(signal[:, :, slot_rows - 2 :], "ctx", 1)
    widened = jnp.concatenate([before, signal], axis=2).astype(f32)
    taps = (widened[:, :, 2:], widened[:, :, 1:-1], widened[:, :, :-2])
    k = kernel[:, :, None, None, :]
    mixture = k[0] * taps[0] + k[1] * taps[1] + k[2] * taps[2]
    hidden = join_sequences((mixture * gate).astype(bf16))
    return hidden, (widened.astype(bf16), gate)


def conv_backward(grad_out, w_out, kernel, stored, slot_rows):
    widened, gate = stored
    widened = widened.astype(f32)
    taps = (widened[:, :, 2:], widened[:, :, 1:-1], widened[:, :, :-2])
    k = kernel[:, :, None, None, :]
    mixture = k[0] * taps[0] + k[1] * taps[1] + k[2] * taps[2]
    grad_hidden = split_sequences(project(grad_out, w_out), slot_rows)
    grad_mix = grad_hidden * gate
    grad_gate = grad_hidden * mixture
    after = from_behind(grad_mix[:, :, :2], "ctx", -1)
    wide = jnp.concatenate([grad_mix, after], axis=2)
    grad_signal = k[0] * grad_mix + k[1] * wide[:, :, 1:-1] + k[2] * wide[:, :, 2:]
    grad_kernel = jnp.stack([jnp.sum(grad_mix * tap, axis=(1, 2)) for tap in taps])
    grad_signal = join_sequences(grad_signal.astype(bf16))
    grad_gate = join_sequences(grad_gate.astype(bf16))
    return grad_signal, grad_gate, grad_kernel


def ffn_forward(normed, w_in):
    z = lax.optimization_barrier(slice_project(normed, w_in).astype(bf16))
    f = z.shape[-1] // 2
    hidden = (jax.nn.silu(z[..., :f].astype(f32)) * z[..., f:].astype(f32)).astype(bf16)
    return hidden, z


def swiglu_grad_kernel(grad_ref, weight_ref, z_ref, out_ref):
    f = weight_ref.shape[1]
    grad_hidden = jnp.dot(grad_ref[...], weight_ref[...], preferred_element_type=f32)
    z = z_ref[...].astype(f32)
    gate, up = z[:, :f], z[:, f:]
    s = 1.0 / (1.0 + jnp.exp(-gate))
    out_ref[:, :f] = (grad_hidden * up * (s * (1.0 + gate * (1.0 - s)))).astype(bf16)
    out_ref[:, f:] = (grad_hidden * (gate * s)).astype(bf16)


def ffn_backward(grad_out, w_out, z):
    count, width = grad_out.shape
    f = w_out.shape[1]
    block = 256
    return pl.pallas_call(
        swiglu_grad_kernel,
        grid=(count // block,),
        in_specs=[
            pl.BlockSpec((block, width), lambda i: (i, 0)),
            pl.BlockSpec((width, f), lambda i: (0, 0)),
            pl.BlockSpec((block, 2 * f), lambda i: (i, 0)),
        ],
        out_specs=pl.BlockSpec((block, 2 * f), lambda i: (i, 0)),
        out_shape=jax.ShapeDtypeStruct((count, 2 * f), bf16),
        cost_estimate=pl.CostEstimate(
            flops=2 * count * width * f,
            bytes_accessed=2 * (count * width + width * f + 4 * count * f),
            transcendentals=count * f,
        ),
        compiler_params=pltpu.CompilerParams(vmem_limit_bytes=56 * 2**20),
    )(grad_out, w_out, z)


def pair_grad_kernel(rows_ref, first_ref, grad_ref, second_ref, out_ref):
    split = first_ref.shape[1]
    down = (((0,), (0,)), ((), ()))
    out_ref[:, :split] = lax.dot_general(
        rows_ref[...], first_ref[...], down, preferred_element_type=f32
    ).astype(bf16)
    out_ref[:, split:] = lax.dot_general(
        grad_ref[...], second_ref[...], down, preferred_element_type=f32
    ).astype(bf16)


def pair_grad(rows, first, grad, second):
    count, width = rows.shape
    groups, a, b = first.shape[0], first.shape[2], second.shape[2]
    block = 256
    return pl.pallas_call(
        pair_grad_kernel,
        grid=(groups, width // block),
        in_specs=[
            pl.BlockSpec((count, block), lambda y, i: (0, i)),
            pl.BlockSpec((None, count, a), lambda y, i: (y, 0, 0)),
            pl.BlockSpec((count, block), lambda y, i: (0, i)),
            pl.BlockSpec((None, count, b), lambda y, i: (y, 0, 0)),
        ],
        out_specs=pl.BlockSpec((None, block, a + b), lambda y, i: (y, i, 0)),
        out_shape=jax.ShapeDtypeStruct((groups, width, a + b), bf16),
        cost_estimate=pl.CostEstimate(
            flops=2 * groups * count * width * (a + b),
            bytes_accessed=2 * groups * (2 * count * width + (count + width) * (a + b)),
            transcendentals=0,
        ),
        compiler_params=pltpu.CompilerParams(vmem_limit_bytes=56 * 2**20),
    )(rows, first, grad, second)


def causal_mask(slot_rows):
    return jnp.arange(slot_rows)[:, None] >= jnp.arange(slot_rows)[None, :]


def to_heads(z, heads):
    y, s, l, width = z.shape
    return z.reshape(y, s, l, heads, width // heads).transpose(0, 1, 3, 2, 4)


def from_heads(value):
    y, s, h, l, e = value.shape
    return value.transpose(0, 1, 3, 2, 4).reshape(y, s * l, h * e)


def attn_forward(normed, w_in, heads, slot_rows):
    z = split_sequences(project(normed, w_in), slot_rows)
    queries = to_heads((0.5 * z[..., : heads * F]).astype(bf16), heads)
    keys = to_heads((0.5 * z[..., heads * F : 2 * heads * F]).astype(bf16), heads)
    values = to_heads(z[..., 2 * heads * F :].astype(bf16), heads)
    extended = jnp.concatenate([values, jnp.ones(values.shape[:-1] + (1,), bf16)], axis=-1)
    k_feat = features(keys.astype(f32)).astype(bf16)
    states = jnp.einsum("...qe,...qv->...ev", k_feat, extended, preferred_element_type=f32)
    earlier = running_sum(states, 1)
    scores = jnp.einsum("...pf,...qf->...pq", queries, keys, preferred_element_type=f32)
    weight = jnp.where(
        causal_mask(slot_rows), 1.0 + scores + 0.5 * scores * scores, 0.0
    ).astype(bf16)
    q_feat = features(queries.astype(f32)).astype(bf16)
    totals = jnp.einsum(
        "...pq,...qv->...pv", weight, extended, preferred_element_type=f32
    ) + jnp.einsum("...pe,...ev->...pv", q_feat, earlier, preferred_element_type=f32)
    out = from_heads((totals[..., :-1] / totals[..., -1:]).astype(bf16))
    return out, (queries, keys, extended, earlier, totals)


def attn_backward(grad_out, w_out, stored, heads, slot_rows):
    (queries, keys, extended, earlier, totals), grad_out = lax.optimization_barrier(
        (stored, grad_out)
    )
    q_feat = features(queries.astype(f32)).astype(bf16)
    k_feat = features(keys.astype(f32)).astype(bf16)
    grad_heads = to_heads(split_sequences(project(grad_out, w_out), slot_rows), heads)
    denominator = totals[..., -1:]
    grad_num = grad_heads / denominator
    grad_den = -jnp.sum(grad_heads * totals[..., :-1], axis=-1, keepdims=True) / (
        denominator * denominator
    )
    grad_total = jnp.concatenate([grad_num, grad_den], axis=-1).astype(bf16)
    grad_prior = jnp.einsum("...pe,...pv->...ev", q_feat, grad_total, preferred_element_type=f32)
    grad_state = running_sum(grad_prior, -1)
    scores = jnp.einsum("...pf,...qf->...pq", queries, keys, preferred_element_type=f32)
    mask = causal_mask(slot_rows)
    weight = jnp.where(mask, 1.0 + scores + 0.5 * scores * scores, 0.0).astype(bf16)
    grad_weight = jnp.einsum("...pv,...qv->...pq", grad_total, extended, preferred_element_type=f32)
    grad_qf = jnp.einsum("...pv,...ev->...pe", grad_total, earlier, preferred_element_type=f32)
    grad_score = jnp.where(mask, grad_weight * (1.0 + scores), 0.0).astype(bf16)
    grad_ext = jnp.einsum(
        "...pq,...pv->...qv", weight, grad_total, preferred_element_type=f32
    ) + jnp.einsum("...qe,...ev->...qv", k_feat, grad_state, preferred_element_type=f32)
    grad_kf = jnp.einsum("...qv,...ev->...qe", extended, grad_state, preferred_element_type=f32)
    unused, pull_query = jax.vjp(features, queries.astype(f32))
    unused, pull_key = jax.vjp(features, keys.astype(f32))
    grad_query = (
        jnp.einsum("...pq,...qf->...pf", grad_score, keys, preferred_element_type=f32)
        + pull_query(grad_qf)[0]
    )
    grad_key = (
        jnp.einsum("...pq,...pf->...qf", grad_score, queries, preferred_element_type=f32)
        + pull_key(grad_kf)[0]
    )
    grad_z = jnp.concatenate(
        [
            from_heads((0.5 * grad_query).astype(bf16)),
            from_heads((0.5 * grad_key).astype(bf16)),
            from_heads(grad_ext[..., :-1].astype(bf16)),
        ],
        axis=-1,
    )
    return grad_z


def norm_back(stream, grad_normed, gain):
    unused, pull = jax.vjp(norm_rows, stream, gain)
    return pull(grad_normed)


def heads_apart(weight):
    d = weight.shape[0]
    return jnp.concatenate(
        [
            weight[..., :F].reshape(d, -1),
            weight[..., F : 2 * F].reshape(d, -1),
            weight[..., 2 * F :].reshape(d, -1),
        ],
        axis=1,
    )


def heads_together(weight, heads):
    d = weight.shape[0]
    q = weight[:, : heads * F].reshape(d, heads, F)
    k = weight[:, heads * F : 2 * heads * F].reshape(d, heads, F)
    v = weight[:, 2 * heads * F :].reshape(d, heads, -1)
    return jnp.concatenate([q, k, v], axis=-1)


def shards(
    hidden_in,
    cotangent,
    lengths,
    to_model,
    to_loader,
    conv_in,
    conv_kernel,
    conv_out,
    ffn_one_in,
    ffn_one_out,
    attn_in,
    attn_out,
    ffn_two_in,
    ffn_two_out,
    gains,
):
    y_size = lax.axis_size("y")
    ctx_size = lax.axis_size("ctx")
    tp_size = 2 * y_size
    group_size = ctx_size * tp_size
    row_count = hidden_in.shape[0]
    per_peer = row_count // group_size
    slot_rows = MAXLEN // ctx_size
    block_rows = row_count * tp_size
    core = lax.axis_index("core")
    tp_rank = lax.axis_index("y") * 2 + core
    heads = attn_in.shape[1]
    rows = Rows(row_count, slot_rows)

    d = conv_in.shape[0]
    conv_width = conv_in.shape[1] * conv_in.shape[2]
    attn_width = heads * attn_in.shape[2]
    attn_start = -(-attn_width // 128) * 128
    c_w = gather_weight(jnp.concatenate([conv_in.reshape(d, -1), conv_out.T], axis=1))
    pad = jnp.zeros((d, attn_start - attn_width), bf16)
    a_w = jnp.concatenate([heads_apart(attn_in), pad, attn_out.T], axis=1)
    ffn_width = ffn_one_in.shape[1] * ffn_one_in.shape[2]
    f1_w = jnp.concatenate([ffn_one_in.reshape(d, -1), ffn_one_out.T], axis=1)
    f2_w = jnp.concatenate([ffn_two_in.reshape(d, -1), ffn_two_out.T], axis=1)

    counter = jnp.arange(row_count, dtype=jnp.int32)
    send_slot = slot_index(to_loader // row_count % group_size, counter, per_peer)
    recv_slot = slot_index(to_model // row_count % group_size, to_model % row_count, per_peer)
    send_order = jnp.argsort(send_slot)
    stream_zero = regroup(hidden_in, send_order, recv_slot)
    f1_w = gather_slice(after(f1_w, c_w, stream_zero))
    a_w = gather_weight(after(a_w, f1_w))
    f2_w = gather_slice(after(f2_w, a_w))
    cotangent = after(cotangent, stream_zero)
    w_c_in, w_c_out = c_w[..., :conv_width], c_w[..., conv_width:]
    w_a_in, w_a_out = a_w[..., :attn_width], a_w[..., attn_start:]
    w_f1_in, w_f1_out = f1_w[:, :ffn_width], f1_w[:, ffn_width:]
    w_f2_in, w_f2_out = f2_w[:, :ffn_width], f2_w[:, ffn_width:]
    cotan_rows = regroup(cotangent, send_order, recv_slot)
    stream_zero = stream_zero.astype(f32)
    seq_lengths = lax.dynamic_index_in_dim(lengths, lax.axis_index("fsdp"), 0, keepdims=False)
    position = lax.axis_index("ctx") * slot_rows + jnp.arange(slot_rows, dtype=jnp.int32)
    valid_block = (position[None, :] < seq_lengths[:, None]).astype(f32).reshape(block_rows)
    valid_rows = lax.dynamic_slice_in_dim(valid_block, tp_rank * row_count, row_count)[:, None]
    channels = conv_in.shape[2]
    kernel = lax.dynamic_index_in_dim(
        conv_kernel.reshape(3, y_size, 2, channels), core, 2, keepdims=False
    )

    def normed_of(stream, index, spread=rows.spread):
        return spread(norm_rows(stream, gains[index]).astype(bf16))

    def grad_rows(carry, spread=rows.spread, *meanwhile):
        return spread((valid_rows * carry).astype(bf16), *meanwhile)

    normed_zero = normed_of(stream_zero, 0)
    hid_zero, stored_zero = conv_forward(normed_zero, w_c_in, kernel, slot_rows)
    stream_one = stream_zero + valid_rows * rows.collect(hid_zero, w_c_out)
    normed_one = normed_of(stream_one, 1, spread_wide)
    upstream = cotan_rows.astype(f32)
    normed_one, grad_out = tie(normed_one, grad_rows(upstream, spread_wide))
    hid_one, z_one = ffn_forward(normed_one, w_f1_in)
    stream_two = stream_one + valid_rows * collect_wide(hid_one, w_f1_out)
    normed_two = normed_of(stream_two, 2)
    hid_two, stored_two = attn_forward(normed_two, w_a_in, heads, slot_rows)
    stream_three = stream_two + valid_rows * rows.collect(hid_two, w_a_out)
    normed_three = normed_of(stream_three, 3, spread_wide)
    hid_three, z_three = ffn_forward(normed_three, w_f2_in)

    grad_z = ffn_backward(grad_out, w_f2_out, z_three)
    g_f2 = pair_grad(normed_three, grad_z[None], grad_out, hid_three[None])[0]
    terms, g_f2 = collect_wide(grad_z, w_f2_in, g_f2)
    step, gain_three = norm_back(stream_three, terms, gains[3])
    upstream = upstream + step
    grad_out = grad_rows(upstream)
    grad_z = attn_backward(grad_out, w_a_out, stored_two, heads, slot_rows)
    g_f2 = scatter_grad(g_f2, LAYER_AXES)
    wide_z = jnp.pad(grad_z, ((0, 0), (0, 0), (0, attn_start - attn_width)))
    g_a = pair_grad(normed_two, wide_z, grad_out, hid_two)
    step, gain_two = norm_back(stream_two, rows.collect(grad_z, w_a_in), gains[2])
    upstream = upstream + step
    upstream, hid_three = tie(upstream, hid_three)
    last_terms = products_wide(hid_three, w_f2_out)
    grad_out, g_a, *last_terms = grad_rows(upstream, spread_wide, g_a, *last_terms)
    g_a = scatter_grad(g_a, WEIGHT_AXES)
    g_a_in, g_a_out = g_a[:, :attn_width], g_a[:, attn_start:]
    out_arrived = reduce_start(grad_out, hid_one)
    grad_z = ffn_backward(grad_out, w_f1_out, z_one)
    in_arrived = reduce_start(normed_one, grad_z)
    step, gain_one = norm_back(stream_one, collect_wide(grad_z, w_f1_in), gains[1])
    upstream = upstream + step
    own_rows = (valid_rows * upstream).astype(bf16)
    own_rows, out_arrived, *last_terms = tie(own_rows, out_arrived, *last_terms)
    last_arrived = swap(last_terms[0], "y", 1)
    stream_four = last_terms[1] + core_swap(last_terms[2]).astype(f32) + last_arrived.astype(f32)
    stream_four = stream_three + valid_rows * stream_four
    hidden_out = regroup(stream_four.astype(bf16), jnp.argsort(recv_slot), send_slot)
    out_parts = reduce_middle(grad_out, hid_one, out_arrived)
    grad_out = rows.spread(own_rows)
    g_c_out = reduce_grad(grad_out, hid_zero, "fsdp")
    grad_signal, grad_gate, grad_kernel = conv_backward(
        grad_out, w_c_out, kernel, stored_zero, slot_rows
    )
    g_c_gate = reduce_grad(normed_zero, grad_gate, "y")
    grad_signal, in_arrived, g_f2, *out_parts = tie(grad_signal, in_arrived, g_f2, *out_parts)
    g_f2_in, g_f2_out = g_f2[:, :ffn_width], g_f2[:, ffn_width:]
    g_f1_out = halve_rest(*out_parts, "ctx").astype(f32)
    g_f1_in = halve_rest(*reduce_middle(normed_one, grad_z, in_arrived), "ctx").astype(f32)
    g_c_signal = reduce_grad(normed_zero, grad_signal, "fsdp")
    grad_z = jnp.concatenate([grad_signal, grad_gate], axis=-1)
    step, gain_zero = norm_back(stream_zero, rows.collect(grad_z, w_c_in), gains[0])
    upstream = upstream + step
    grad_in = regroup(upstream.astype(bf16), jnp.argsort(recv_slot), send_slot)

    kernel_full = jnp.where(
        (jnp.arange(2) == core)[None, None, :, None], grad_kernel[:, :, None, :], 0.0
    ).reshape(conv_kernel.shape)
    gain_stack = jnp.stack([gain_zero, gain_one, gain_two, gain_three])
    summed = sum_everywhere(jnp.concatenate([gain_stack, kernel_full], axis=0))
    return (
        hidden_out,
        grad_in,
        jnp.stack([g_c_signal, g_c_gate], axis=1),
        summed[4:],
        g_c_out.T,
        g_f1_in.reshape(ffn_one_in.shape),
        g_f1_out.T,
        heads_together(g_a_in, heads),
        g_a_out.T,
        g_f2_in.reshape(ffn_two_in.shape),
        g_f2_out.T,
        summed[:4],
    )


def solution(mesh):
    fsdp, ctx, tp = mesh.devices.shape
    fine = Mesh(mesh.devices.reshape(fsdp, ctx, tp // 2, 2), ("fsdp", "ctx", "y", "core"))
    everything = ("fsdp", "ctx", "y", "core")
    layer = ("fsdp", "ctx")
    tensor = ("y", "core")
    ins = (
        P(everything, None),
        P(everything, None),
        P(),
        P(everything),
        P(everything),
        P(layer, None, tensor),
        P(),
        P(tensor, layer),
        P(layer, None, tensor),
        P(tensor, layer),
        P(layer, tensor, None),
        P(tensor, layer),
        P(layer, None, tensor),
        P(tensor, layer),
        P(),
    )
    outs = (
        P(everything, None),
        P(everything, None),
        P(layer, None, tensor),
        P(),
        P(tensor, layer),
        P(layer, None, tensor),
        P(tensor, layer),
        P(layer, tensor, None),
        P(tensor, layer),
        P(layer, None, tensor),
        P(tensor, layer),
        P(),
    )
    return jax.shard_map(shards, mesh=fine, in_specs=ins, out_specs=outs, check_vma=False)
```

```python
import jax
import jax.numpy as jnp
import numpy as np
from jax import lax
from jax.experimental import pallas as pl
from jax.experimental.pallas import tpu as pltpu
from jax.sharding import Mesh, PartitionSpec as P

F = 16
MAXLEN = 2048

epsilon = 1e-05
quad_scale = 0.7071067811865476
WEIGHT_AXES = ("y", "fsdp", "ctx")
LAYER_AXES = ("fsdp", "ctx")
bf16 = jnp.bfloat16
f32 = jnp.float32


def from_behind(block, axis, distance):
    devices = range(lax.axis_size(axis))
    route = [(i - distance, i) for i in devices if i - distance in devices]
    return lax.ppermute(block, axis, route)


def running_sum(part, direction):
    window = part
    total = jnp.zeros(part.shape, f32)
    step = 1
    while step < lax.axis_size("ctx"):
        arrived = from_behind(window.astype(bf16), "ctx", direction * step).astype(f32)
        total = total + arrived
        window = window + arrived
        step *= 2
    return (total * TIMES[:, None]).astype(bf16)


def sum_everywhere(value):
    for axis in ("core", "y", "fsdp", "ctx"):
        step = 1
        size = lax.axis_size(axis)
        while step < size:
            value = value + lax.ppermute(value, axis, [(i, i ^ step) for i in range(size)])
            step *= 2
    return value


PAIRS = [(a, b) for a in range(F) for b in range(a, F)]
FIRST = np.array([[float(a == i) for a, b in PAIRS] for i in range(F)], np.float32)
SECOND = np.array([[float(b == i) for a, b in PAIRS] for i in range(F)], np.float32)
TIMES = np.array([2.0 if a < b else 1.0 for a, b in PAIRS] + [1.0] * (F + 1), np.float32)


def features(vector):
    quad = jnp.dot(vector, FIRST) * jnp.dot(vector, SECOND) * quad_scale
    return jnp.concatenate([quad, vector, jnp.ones(vector.shape[:-1] + (1,), f32)], axis=-1)


def norm_rows(stream, gain):
    return stream * lax.rsqrt(jnp.mean(stream * stream, axis=-1, keepdims=True) + epsilon) * gain


def slot_index(peer, order_key, per_peer):
    same = peer[:, None] == peer[None, :]
    before = order_key[None, :] < order_key[:, None]
    return peer * per_peer + jnp.sum((same & before).astype(jnp.int32), axis=1)


def regroup(rows, order, position):
    received = lax.all_to_all(
        rows[order], ("ctx", "y", "core"), split_axis=0, concat_axis=0, tiled=True
    )
    return received[position]


def core_swap(value):
    return lax.ppermute(value, "core", [(0, 1), (1, 0)])


def gather_weight(weight):
    whole = lax.all_gather(weight, WEIGHT_AXES, axis=0, tiled=True)
    return whole.reshape(lax.axis_size("y"), -1, weight.shape[1])


def gather_slice(weight):
    return lax.all_gather(weight, LAYER_AXES, axis=0, tiled=True)


def scatter_grad(grad, axes):
    flat = grad.astype(bf16).reshape(-1, grad.shape[-1])
    return lax.psum_scatter(flat, axes, scatter_dimension=0, tiled=True).astype(f32)


def tie(*values):
    return lax.optimization_barrier(values)


def after(value, *others):
    for other in others:
        corner = other.reshape((-1,) + other.shape[-2:])[0, :16, :128]
        first = lax.optimization_barrier(corner)[:1, :1].reshape(())
        value = value + (first * 0).astype(value.dtype)
    return value


def bit_of(axis, step):
    return lax.axis_index(axis) // step % 2


def swap(value, axis, step):
    return lax.ppermute(value, axis, [(i, i ^ step) for i in range(lax.axis_size(axis))])


def pick(value, index, dim):
    return lax.dynamic_index_in_dim(value, index, dim, keepdims=False)


def halve_start(value, axis):
    size = lax.axis_size(axis)
    dims = size.bit_length() - 1
    value = value.reshape((2,) * dims + value.shape[1:])
    bit = bit_of(axis, 1)
    return pick(value, bit, dims - 1), swap(pick(value, 1 - bit, dims - 1), axis, 1)


def halve_rest(kept, arrived, axis):
    size = lax.axis_size(axis) // 2
    value = (kept.astype(f32) + arrived.astype(f32)).astype(bf16)
    dims = size.bit_length() - 1
    return halve(value.reshape((size,) + value.shape[dims:]), axis, 2)


def halve(value, axis, done=1):
    size = lax.axis_size(axis) // done
    dims = size.bit_length() - 1
    value = value.reshape((2,) * dims + value.shape[1:])
    for dim in reversed(range(dims)):
        bit = bit_of(axis, done)
        other = swap(pick(value, 1 - bit, dim), axis, done)
        value = (pick(value, bit, dim).astype(f32) + other.astype(f32)).astype(bf16)
        done *= 2
    return value


def half_columns(rows, bit, fsdp):
    width = rows.shape[1] // fsdp
    if fsdp == 2:
        return lax.dynamic_slice_in_dim(rows, bit * width, width, 1)
    parts = rows.reshape(-1, fsdp // 2, 2, width)
    return pick(parts, bit, 2).reshape(-1, fsdp // 2 * width)


def reduce_start(rows, value):
    fsdp = lax.axis_size("fsdp")
    theirs = slice_grad(half_columns(rows, 1 - bit_of("fsdp", 1), fsdp), value)
    return swap(theirs.astype(bf16), "fsdp", 1)


def reduce_middle(rows, value, arrived):
    fsdp, ctx = (lax.axis_size(axis) for axis in LAYER_AXES)
    k = value.shape[-1]
    mine = slice_grad(half_columns(rows, bit_of("fsdp", 1), fsdp), value)
    total = (mine + arrived.astype(f32)).astype(bf16)
    total = halve(total.reshape(fsdp // 2, ctx, -1, k), "fsdp", 2)
    return halve_start(total, "ctx")


def reduce_grad(rows, value, first):
    fsdp, ctx, y = (lax.axis_size(axis) for axis in ("fsdp", "ctx", "y"))
    k = value.shape[-1]
    d = rows.shape[1] // (fsdp * ctx)
    bit = bit_of(first, 1)
    if first == "y":
        parts = value.reshape(y // 2, 2, -1, k)
        theirs = weight_grad(rows, pick(parts, 1 - bit, 1)).astype(bf16)
        mine = weight_grad(rows, pick(parts, bit, 1))
    else:
        theirs = weight_grad(half_columns(rows, 1 - bit, fsdp), value)
        mine = weight_grad(half_columns(rows, bit, fsdp), value)
        theirs = theirs.astype(bf16)
    total = (mine + swap(theirs, first, 1).astype(f32)).astype(bf16)
    if first == "y":
        total = halve(total.reshape(y // 2, fsdp, ctx, d, k), "y", 2)
        total = halve(total, "fsdp")
    else:
        total = total.reshape(y, fsdp // 2, ctx, d, k).swapaxes(0, 1)
        total = halve(halve(total, "fsdp", 2), "y")
    return halve(total, "ctx").astype(f32)


class Rows:
    def __init__(self, row_count, slot_rows):
        self.count = row_count
        self.own_first = row_count % slot_rows == 0
        self.core = lax.axis_index("core")

    def spread(self, own):
        other = core_swap(own)
        if self.own_first:
            return jnp.concatenate([own, other], axis=0)
        low = jnp.where(self.core == 0, own, other)
        high = jnp.where(self.core == 0, other, own)
        return jnp.concatenate([low, high], axis=0)

    def halves(self, value):
        if self.own_first:
            return value[:, : self.count], value[:, self.count :]
        own = lax.dynamic_slice_in_dim(value, self.core * self.count, self.count, 1)
        other = lax.dynamic_slice_in_dim(value, (1 - self.core) * self.count, self.count, 1)
        return own, other

    def collect(self, value, weight):
        own, other = self.halves(value)
        theirs = jnp.einsum("yrk,ydk->rd", other, weight, preferred_element_type=f32).astype(bf16)
        arrived = core_swap(theirs)
        mine = jnp.einsum("yrk,ydk->rd", own, weight, preferred_element_type=f32)
        return mine + arrived.astype(f32)


def spread_wide(own, *meanwhile):
    value = own[None]
    step = 1
    while step < lax.axis_size("y"):
        arrived, *meanwhile = tie(swap(value, "y", step), *meanwhile)
        value = jnp.concatenate([value, arrived], axis=0)
        step *= 2
    other = core_swap(value)
    value = jnp.concatenate([value, other], axis=0).reshape(-1, own.shape[-1])
    return (value, *meanwhile) if meanwhile else value


def products_wide(value, weight):
    y = lax.axis_size("y")
    blocks = value.reshape(2, y, -1, value.shape[-1])
    count = blocks.shape[2]

    def part(block):
        flat = block.reshape(-1, block.shape[-1])
        return jnp.einsum("rk,dk->rd", flat, weight, preferred_element_type=f32)

    far = part(blocks[:, 1:]).reshape(2, y - 1, count, -1)
    far = far[0] + core_swap(far[1].astype(bf16)).astype(f32)
    extra = 0.0
    step = y // 2
    while step > 1:
        arrived = swap(far[step - 1 :].astype(bf16), "y", step).astype(f32)
        extra = extra + arrived[0]
        far = far[: step - 1] + arrived[1:]
        step //= 2
    near = part(blocks[:, 0]).reshape(2, count, -1)
    return far[0].astype(bf16), near[0] + extra, near[1].astype(bf16)


def collect_wide(value, weight, *meanwhile):
    far, near, neighbour = products_wide(value, weight)
    arrived, near, neighbour, *meanwhile = tie(swap(far, "y", 1), near, neighbour, *meanwhile)
    total = near + core_swap(neighbour).astype(f32) + arrived.astype(f32)
    return (total, *meanwhile) if meanwhile else total


def slice_project(rows, weight):
    return jnp.einsum("rd,dk->rk", rows, weight, preferred_element_type=f32)


def slice_grad(rows, value):
    return jnp.einsum("rd,rk->dk", rows, value, preferred_element_type=f32)


def project(normed, weight):
    return jnp.einsum("rd,ydk->yrk", normed, weight, preferred_element_type=f32)


def weight_grad(rows, value):
    return jnp.einsum("rd,yrk->ydk", rows, value, preferred_element_type=f32)


def split_sequences(value, slot_rows):
    return value.reshape(value.shape[0], -1, slot_rows, value.shape[-1])


def join_sequences(value):
    return value.reshape(value.shape[0], -1, value.shape[-1])


def conv_forward(normed, w_in, kernel, slot_rows):
    z = split_sequences(project(normed, w_in), slot_rows)
    ch = z.shape[-1] // 2
    signal = z[..., :ch].astype(bf16)
    gate = z[..., ch:]
    before = from_behind(signal[:, :, slot_rows - 2 :], "ctx", 1)
    widened = jnp.concatenate([before, signal], axis=2).astype(f32)
    taps = (widened[:, :, 2:], widened[:, :, 1:-1], widened[:, :, :-2])
    k = kernel[:, :, None, None, :]
    mixture = k[0] * taps[0] + k[1] * taps[1] + k[2] * taps[2]
    hidden = join_sequences((mixture * gate).astype(bf16))
    return hidden, (widened.astype(bf16), gate)


def conv_backward(grad_out, w_out, kernel, stored, slot_rows):
    widened, gate = stored
    widened = widened.astype(f32)
    taps = (widened[:, :, 2:], widened[:, :, 1:-1], widened[:, :, :-2])
    k = kernel[:, :, None, None, :]
    mixture = k[0] * taps[0] + k[1] * taps[1] + k[2] * taps[2]
    grad_hidden = split_sequences(project(grad_out, w_out), slot_rows)
    grad_mix = grad_hidden * gate
    grad_gate = grad_hidden * mixture
    after = from_behind(grad_mix[:, :, :2], "ctx", -1)
    wide = jnp.concatenate([grad_mix, after], axis=2)
    grad_signal = k[0] * grad_mix + k[1] * wide[:, :, 1:-1] + k[2] * wide[:, :, 2:]
    grad_kernel = jnp.stack([jnp.sum(grad_mix * tap, axis=(1, 2)) for tap in taps])
    grad_signal = join_sequences(grad_signal.astype(bf16))
    grad_gate = join_sequences(grad_gate.astype(bf16))
    return grad_signal, grad_gate, grad_kernel


def ffn_forward(normed, w_in):
    z = lax.optimization_barrier(slice_project(normed, w_in).astype(bf16))
    f = z.shape[-1] // 2
    hidden = (jax.nn.silu(z[..., :f].astype(f32)) * z[..., f:].astype(f32)).astype(bf16)
    return hidden, z


def swiglu_grad_kernel(grad_ref, weight_ref, z_ref, out_ref):
    f = weight_ref.shape[1]
    grad_hidden = jnp.dot(grad_ref[...], weight_ref[...], preferred_element_type=f32)
    z = z_ref[...].astype(f32)
    gate, up = z[:, :f], z[:, f:]
    s = 1.0 / (1.0 + jnp.exp(-gate))
    out_ref[:, :f] = (grad_hidden * up * (s * (1.0 + gate * (1.0 - s)))).astype(bf16)
    out_ref[:, f:] = (grad_hidden * (gate * s)).astype(bf16)


def ffn_backward(grad_out, w_out, z):
    count, width = grad_out.shape
    f = w_out.shape[1]
    block = 256
    return pl.pallas_call(
        swiglu_grad_kernel,
        grid=(count // block,),
        in_specs=[
            pl.BlockSpec((block, width), lambda i: (i, 0)),
            pl.BlockSpec((width, f), lambda i: (0, 0)),
            pl.BlockSpec((block, 2 * f), lambda i: (i, 0)),
        ],
        out_specs=pl.BlockSpec((block, 2 * f), lambda i: (i, 0)),
        out_shape=jax.ShapeDtypeStruct((count, 2 * f), bf16),
        cost_estimate=pl.CostEstimate(
            flops=2 * count * width * f,
            bytes_accessed=2 * (count * width + width * f + 4 * count * f),
            transcendentals=count * f,
        ),
        compiler_params=pltpu.CompilerParams(vmem_limit_bytes=56 * 2**20),
    )(grad_out, w_out, z)


def pair_grad_kernel(rows_ref, first_ref, grad_ref, second_ref, out_ref):
    split = first_ref.shape[1]
    down = (((0,), (0,)), ((), ()))
    out_ref[:, :split] = lax.dot_general(
        rows_ref[...], first_ref[...], down, preferred_element_type=f32
    ).astype(bf16)
    out_ref[:, split:] = lax.dot_general(
        grad_ref[...], second_ref[...], down, preferred_element_type=f32
    ).astype(bf16)


def pair_grad(rows, first, grad, second):
    count, width = rows.shape
    groups, a, b = first.shape[0], first.shape[2], second.shape[2]
    block = 256
    return pl.pallas_call(
        pair_grad_kernel,
        grid=(groups, width // block),
        in_specs=[
            pl.BlockSpec((count, block), lambda y, i: (0, i)),
            pl.BlockSpec((None, count, a), lambda y, i: (y, 0, 0)),
            pl.BlockSpec((count, block), lambda y, i: (0, i)),
            pl.BlockSpec((None, count, b), lambda y, i: (y, 0, 0)),
        ],
        out_specs=pl.BlockSpec((None, block, a + b), lambda y, i: (y, i, 0)),
        out_shape=jax.ShapeDtypeStruct((groups, width, a + b), bf16),
        cost_estimate=pl.CostEstimate(
            flops=2 * groups * count * width * (a + b),
            bytes_accessed=2 * groups * (2 * count * width + (count + width) * (a + b)),
            transcendentals=0,
        ),
        compiler_params=pltpu.CompilerParams(vmem_limit_bytes=56 * 2**20),
    )(rows, first, grad, second)


def causal_mask(slot_rows):
    return jnp.arange(slot_rows)[:, None] >= jnp.arange(slot_rows)[None, :]


def to_heads(z, heads):
    y, s, l, width = z.shape
    return z.reshape(y, s, l, heads, width // heads).transpose(0, 1, 3, 2, 4)


def from_heads(value):
    y, s, h, l, e = value.shape
    return value.transpose(0, 1, 3, 2, 4).reshape(y, s * l, h * e)


def attn_forward(normed, w_in, heads, slot_rows):
    z = split_sequences(project(normed, w_in), slot_rows)
    queries = to_heads((0.5 * z[..., : heads * F]).astype(bf16), heads)
    keys = to_heads((0.5 * z[..., heads * F : 2 * heads * F]).astype(bf16), heads)
    values = to_heads(z[..., 2 * heads * F :].astype(bf16), heads)
    extended = jnp.concatenate([values, jnp.ones(values.shape[:-1] + (1,), bf16)], axis=-1)
    k_feat = features(keys.astype(f32)).astype(bf16)
    states = jnp.einsum("...qe,...qv->...ev", k_feat, extended, preferred_element_type=f32)
    earlier = running_sum(states, 1)
    scores = jnp.einsum("...pf,...qf->...pq", queries, keys, preferred_element_type=f32)
    weight = jnp.where(
        causal_mask(slot_rows), 1.0 + scores + 0.5 * scores * scores, 0.0
    ).astype(bf16)
    q_feat = features(queries.astype(f32)).astype(bf16)
    totals = jnp.einsum(
        "...pq,...qv->...pv", weight, extended, preferred_element_type=f32
    ) + jnp.einsum("...pe,...ev->...pv", q_feat, earlier, preferred_element_type=f32)
    out = from_heads((totals[..., :-1] / totals[..., -1:]).astype(bf16))
    return out, (queries, keys, extended, earlier, totals)


def attn_backward(grad_out, w_out, stored, heads, slot_rows):
    (queries, keys, extended, earlier, totals), grad_out = lax.optimization_barrier(
        (stored, grad_out)
    )
    q_feat = features(queries.astype(f32)).astype(bf16)
    k_feat = features(keys.astype(f32)).astype(bf16)
    grad_heads = to_heads(split_sequences(project(grad_out, w_out), slot_rows), heads)
    denominator = totals[..., -1:]
    grad_num = grad_heads / denominator
    grad_den = -jnp.sum(grad_heads * totals[..., :-1], axis=-1, keepdims=True) / (
        denominator * denominator
    )
    grad_total = jnp.concatenate([grad_num, grad_den], axis=-1).astype(bf16)
    grad_prior = jnp.einsum("...pe,...pv->...ev", q_feat, grad_total, preferred_element_type=f32)
    grad_state = running_sum(grad_prior, -1)
    scores = jnp.einsum("...pf,...qf->...pq", queries, keys, preferred_element_type=f32)
    mask = causal_mask(slot_rows)
    weight = jnp.where(mask, 1.0 + scores + 0.5 * scores * scores, 0.0).astype(bf16)
    grad_weight = jnp.einsum("...pv,...qv->...pq", grad_total, extended, preferred_element_type=f32)
    grad_qf = jnp.einsum("...pv,...ev->...pe", grad_total, earlier, preferred_element_type=f32)
    grad_score = jnp.where(mask, grad_weight * (1.0 + scores), 0.0).astype(bf16)
    grad_ext = jnp.einsum(
        "...pq,...pv->...qv", weight, grad_total, preferred_element_type=f32
    ) + jnp.einsum("...qe,...ev->...qv", k_feat, grad_state, preferred_element_type=f32)
    grad_kf = jnp.einsum("...qv,...ev->...qe", extended, grad_state, preferred_element_type=f32)
    unused, pull_query = jax.vjp(features, queries.astype(f32))
    unused, pull_key = jax.vjp(features, keys.astype(f32))
    grad_query = (
        jnp.einsum("...pq,...qf->...pf", grad_score, keys, preferred_element_type=f32)
        + pull_query(grad_qf)[0]
    )
    grad_key = (
        jnp.einsum("...pq,...pf->...qf", grad_score, queries, preferred_element_type=f32)
        + pull_key(grad_kf)[0]
    )
    grad_z = jnp.concatenate(
        [
            from_heads((0.5 * grad_query).astype(bf16)),
            from_heads((0.5 * grad_key).astype(bf16)),
            from_heads(grad_ext[..., :-1].astype(bf16)),
        ],
        axis=-1,
    )
    return grad_z


def norm_back(stream, grad_normed, gain):
    unused, pull = jax.vjp(norm_rows, stream, gain)
    return pull(grad_normed)


def heads_apart(weight):
    d = weight.shape[0]
    return jnp.concatenate(
        [
            weight[..., :F].reshape(d, -1),
            weight[..., F : 2 * F].reshape(d, -1),
            weight[..., 2 * F :].reshape(d, -1),
        ],
        axis=1,
    )


def heads_together(weight, heads):
    d = weight.shape[0]
    q = weight[:, : heads * F].reshape(d, heads, F)
    k = weight[:, heads * F : 2 * heads * F].reshape(d, heads, F)
    v = weight[:, 2 * heads * F :].reshape(d, heads, -1)
    return jnp.concatenate([q, k, v], axis=-1)


def shards(
    hidden_in,
    cotangent,
    lengths,
    to_model,
    to_loader,
    conv_in,
    conv_kernel,
    conv_out,
    ffn_one_in,
    ffn_one_out,
    attn_in,
    attn_out,
    ffn_two_in,
    ffn_two_out,
    gains,
):
    y_size = lax.axis_size("y")
    ctx_size = lax.axis_size("ctx")
    tp_size = 2 * y_size
    group_size = ctx_size * tp_size
    row_count = hidden_in.shape[0]
    per_peer = row_count // group_size
    slot_rows = MAXLEN // ctx_size
    block_rows = row_count * tp_size
    core = lax.axis_index("core")
    tp_rank = lax.axis_index("y") * 2 + core
    heads = attn_in.shape[1]
    rows = Rows(row_count, slot_rows)

    d = conv_in.shape[0]
    conv_width = conv_in.shape[1] * conv_in.shape[2]
    attn_width = heads * attn_in.shape[2]
    attn_start = -(-attn_width // 128) * 128
    c_w = gather_weight(jnp.concatenate([conv_in.reshape(d, -1), conv_out.T], axis=1))
    pad = jnp.zeros((d, attn_start - attn_width), bf16)
    a_w = jnp.concatenate([heads_apart(attn_in), pad, attn_out.T], axis=1)
    ffn_width = ffn_one_in.shape[1] * ffn_one_in.shape[2]
    f1_w = jnp.concatenate([ffn_one_in.reshape(d, -1), ffn_one_out.T], axis=1)
    f2_w = jnp.concatenate([ffn_two_in.reshape(d, -1), ffn_two_out.T], axis=1)

    counter = jnp.arange(row_count, dtype=jnp.int32)
    send_slot = slot_index(to_loader // row_count % group_size, counter, per_peer)
    recv_slot = slot_index(to_model // row_count % group_size, to_model % row_count, per_peer)
    send_order = jnp.argsort(send_slot)
    stream_zero = regroup(hidden_in, send_order, recv_slot)
    f1_w = gather_slice(after(f1_w, c_w, stream_zero))
    a_w = gather_weight(after(a_w, f1_w))
    f2_w = gather_slice(after(f2_w, a_w))
    cotangent = after(cotangent, stream_zero)
    w_c_in, w_c_out = c_w[..., :conv_width], c_w[..., conv_width:]
    w_a_in, w_a_out = a_w[..., :attn_width], a_w[..., attn_start:]
    w_f1_in, w_f1_out = f1_w[:, :ffn_width], f1_w[:, ffn_width:]
    w_f2_in, w_f2_out = f2_w[:, :ffn_width], f2_w[:, ffn_width:]
    cotan_rows = regroup(cotangent, send_order, recv_slot)
    stream_zero = stream_zero.astype(f32)
    seq_lengths = lax.dynamic_index_in_dim(lengths, lax.axis_index("fsdp"), 0, keepdims=False)
    position = lax.axis_index("ctx") * slot_rows + jnp.arange(slot_rows, dtype=jnp.int32)
    valid_block = (position[None, :] < seq_lengths[:, None]).astype(f32).reshape(block_rows)
    valid_rows = lax.dynamic_slice_in_dim(valid_block, tp_rank * row_count, row_count)[:, None]
    channels = conv_in.shape[2]
    kernel = lax.dynamic_index_in_dim(
        conv_kernel.reshape(3, y_size, 2, channels), core, 2, keepdims=False
    )

    def normed_of(stream, index, spread=rows.spread):
        return spread(norm_rows(stream, gains[index]).astype(bf16))

    def grad_rows(carry, spread=rows.spread, *meanwhile):
        return spread((valid_rows * carry).astype(bf16), *meanwhile)

    normed_zero = normed_of(stream_zero, 0)
    hid_zero, stored_zero = conv_forward(normed_zero, w_c_in, kernel, slot_rows)
    stream_one = stream_zero + valid_rows * rows.collect(hid_zero, w_c_out)
    normed_one = normed_of(stream_one, 1, spread_wide)
    upstream = cotan_rows.astype(f32)
    normed_one, grad_out = tie(normed_one, grad_rows(upstream, spread_wide))
    hid_one, z_one = ffn_forward(normed_one, w_f1_in)
    stream_two = stream_one + valid_rows * collect_wide(hid_one, w_f1_out)
    normed_two = normed_of(stream_two, 2)
    hid_two, stored_two = attn_forward(normed_two, w_a_in, heads, slot_rows)
    stream_three = stream_two + valid_rows * rows.collect(hid_two, w_a_out)
    normed_three = normed_of(stream_three, 3, spread_wide)
    hid_three, z_three = ffn_forward(normed_three, w_f2_in)

    grad_z = ffn_backward(grad_out, w_f2_out, z_three)
    g_f2 = pair_grad(normed_three, grad_z[None], grad_out, hid_three[None])[0]
    terms, g_f2 = collect_wide(grad_z, w_f2_in, g_f2)
    step, gain_three = norm_back(stream_three, terms, gains[3])
    upstream = upstream + step
    grad_out = grad_rows(upstream)
    grad_z = attn_backward(grad_out, w_a_out, stored_two, heads, slot_rows)
    g_f2 = scatter_grad(g_f2, LAYER_AXES)
    g_f2_in, g_f2_out = g_f2[:, :ffn_width], g_f2[:, ffn_width:]
    wide_z = jnp.pad(grad_z, ((0, 0), (0, 0), (0, attn_start - attn_width)))
    g_a = pair_grad(normed_two, wide_z, grad_out, hid_two)
    step, gain_two = norm_back(stream_two, rows.collect(grad_z, w_a_in), gains[2])
    upstream = upstream + step
    upstream, hid_three = tie(upstream, hid_three)
    last_terms = products_wide(hid_three, w_f2_out)
    grad_out, g_a, *last_terms = grad_rows(upstream, spread_wide, g_a, *last_terms)
    g_a = scatter_grad(g_a, WEIGHT_AXES)
    g_a_in, g_a_out = g_a[:, :attn_width], g_a[:, attn_start:]
    out_arrived = reduce_start(grad_out, hid_one)
    grad_z = ffn_backward(grad_out, w_f1_out, z_one)
    in_arrived = reduce_start(normed_one, grad_z)
    step, gain_one = norm_back(stream_one, collect_wide(grad_z, w_f1_in), gains[1])
    upstream = upstream + step
    own_rows = (valid_rows * upstream).astype(bf16)
    own_rows, out_arrived, *last_terms = tie(own_rows, out_arrived, *last_terms)
    last_arrived = swap(last_terms[0], "y", 1)
    stream_four = last_terms[1] + core_swap(last_terms[2]).astype(f32) + last_arrived.astype(f32)
    stream_four = stream_three + valid_rows * stream_four
    hidden_out = regroup(stream_four.astype(bf16), jnp.argsort(recv_slot), send_slot)
    out_parts = reduce_middle(grad_out, hid_one, out_arrived)
    grad_out = rows.spread(own_rows)
    g_c_out = reduce_grad(grad_out, hid_zero, "fsdp")
    grad_signal, grad_gate, grad_kernel = conv_backward(
        grad_out, w_c_out, kernel, stored_zero, slot_rows
    )
    g_c_gate = reduce_grad(normed_zero, grad_gate, "y")
    grad_signal, in_arrived, *out_parts = tie(grad_signal, in_arrived, *out_parts)
    g_f1_out = halve_rest(*out_parts, "ctx").astype(f32)
    g_f1_in = halve_rest(*reduce_middle(normed_one, grad_z, in_arrived), "ctx").astype(f32)
    g_c_signal = reduce_grad(normed_zero, grad_signal, "fsdp")
    grad_z = jnp.concatenate([grad_signal, grad_gate], axis=-1)
    step, gain_zero = norm_back(stream_zero, rows.collect(grad_z, w_c_in), gains[0])
    upstream = upstream + step
    grad_in = regroup(upstream.astype(bf16), jnp.argsort(recv_slot), send_slot)

    kernel_full = jnp.where(
        (jnp.arange(2) == core)[None, None, :, None], grad_kernel[:, :, None, :], 0.0
    ).reshape(conv_kernel.shape)
    gain_stack = jnp.stack([gain_zero, gain_one, gain_two, gain_three])
    summed = sum_everywhere(jnp.concatenate([gain_stack, kernel_full], axis=0))
    return (
        hidden_out,
        grad_in,
        jnp.stack([g_c_signal, g_c_gate], axis=1),
        summed[4:],
        g_c_out.T,
        g_f1_in.reshape(ffn_one_in.shape),
        g_f1_out.T,
        heads_together(g_a_in, heads),
        g_a_out.T,
        g_f2_in.reshape(ffn_two_in.shape),
        g_f2_out.T,
        summed[:4],
    )


def solution(mesh):
    fsdp, ctx, tp = mesh.devices.shape
    fine = Mesh(mesh.devices.reshape(fsdp, ctx, tp // 2, 2), ("fsdp", "ctx", "y", "core"))
    everything = ("fsdp", "ctx", "y", "core")
    layer = ("fsdp", "ctx")
    tensor = ("y", "core")
    ins = (
        P(everything, None),
        P(everything, None),
        P(),
        P(everything),
        P(everything),
        P(layer, None, tensor),
        P(),
        P(tensor, layer),
        P(layer, None, tensor),
        P(tensor, layer),
        P(layer, tensor, None),
        P(tensor, layer),
        P(layer, None, tensor),
        P(tensor, layer),
        P(),
    )
    outs = (
        P(everything, None),
        P(everything, None),
        P(layer, None, tensor),
        P(),
        P(tensor, layer),
        P(layer, None, tensor),
        P(tensor, layer),
        P(layer, tensor, None),
        P(tensor, layer),
        P(layer, None, tensor),
        P(tensor, layer),
        P(),
    )
    return jax.shard_map(shards, mesh=fine, in_specs=ins, out_specs=outs, check_vma=False)
```
